256 devices in a mesh: dp: 32 (over x, z), seq: 8 (over y, core).
Axes of the slice: x: 4, y: 4, z: 8, core: 2. Of those that a mesh axis runs over, the one named last changes fastest.
Arguments:
- queries: bfloat16 [65536, 4096], P(('dp', 'seq')), may hold values from -8 to 8
- keys: bfloat16 [65536, 1024], P(('dp', 'seq')), may hold values from -8 to 8
- values: bfloat16 [65536, 1024], P(('dp', 'seq')), may hold values from -6 to 6
- row_offsets: int32 [256, 32], replicated, may hold values from 0 to 256, as said below
- doc_lengths: int32 [32, 32], replicated, may hold values from 0 to 2048, as said below
Outputs:
- attended: bfloat16 [65536, 4096], P(('dp', 'seq'))
The draws below stay inside these ranges and needn't reach their ends.
Inputs may be any that keep to these rules, and one draw needn't show every extreme that they name: row_offsets[d * 8 + s, g] is the first local row of loader device (d, s) that belongs to group g; a device's rows are ordered by group, so group g's rows run up to the next group's start, or to 256 for the last group. At most 16 rows of one device belong to one group, and the devices (d, s) of one s hold at most 384 rows of one group together; both bounds are reached in every draw. `doc_lengths`: row g lists the lengths of group g's documents in stream order, then zeros; they sum to the number of rows that belong to group g. Every document but a group's last has 128 to 2048 tokens, a group's last has 1 to 2048; some document has exactly 2048.
All inputs are finite; a program needn't handle non-finite values.
Results may differ from the reference program's by a relative error of at most 0.0036.
Values may be sent and summed in bfloat16 or wider, within the bound.
A program may use at most 64 MiB of HBM per device.

```python
import jax
import jax.numpy as jnp
from jax import lax

QUERY_HEADS = 32
KEY_VALUE_HEADS = 8
HEAD_DIMENSION = 128
TOK_DEV = 256
DOCS_G = 32
TOTAL_TOKENS = 65536
ROWS_MAX = 384
DOC_MAX = 2048
DOC_MIN = 128
N_DP = 32
N_SEQ = 8


def group_counts(key):
    key = jax.random.fold_in(key, 101)
    half_count = N_DP // 2
    unit_rows = TOK_DEV // N_DP
    tables = []
    for seq_number in range(N_SEQ):
        seq_key = jax.random.fold_in(key, seq_number + 1)
        key_a, key_b, random_key_third = jax.random.split(seq_key, 3)
        group_rank = jnp.argsort(jax.random.permutation(key_a, N_DP))
        row_rank = jnp.argsort(jax.random.permutation(key_b, N_DP))
        heavy_group = group_rank < half_count
        in_rows = row_rank < half_count
        pair_id = jnp.clip(group_rank - half_count, 0, N_DP) // 2
        pair_sign = jnp.where((group_rank - half_count) % 2 == 0, 1, -1)
        jitter = jax.random.randint(random_key_third, (N_DP, half_count // 2), 0, unit_rows + 1)
        light_term = jnp.where(heavy_group[None, :], 0, pair_sign[None, :] * jnp.take(jitter, pair_id, axis=1))
        skewed = jnp.where(heavy_group[None, :], unit_rows, -unit_rows)
        table = unit_rows + jnp.where(in_rows[:, None], skewed + 0 * light_term, light_term)
        tables.append(jnp.reshape(table, (N_DP, N_DP)))
    per_seq = jnp.reshape(jnp.stack(tables, axis=0), (N_SEQ, N_DP, N_DP))
    return jnp.transpose(per_seq, (1, 0, 2)).reshape(N_DP * N_SEQ, N_DP).astype(jnp.int32)


def draw_row_offsets(key, part):
    counts = group_counts(key)
    return (jnp.cumsum(counts, axis=1) - counts).astype(jnp.int32)


def draw_doc_lengths(key, part):
    counts = group_counts(key)
    key = jax.random.fold_in(key, 7)
    totals = jnp.sum(counts, axis=0)
    pieces = jax.random.randint(key, (N_DP, DOCS_G), DOC_MIN, DOC_MAX // 2 + 1)
    fullest = jnp.argmax(totals)
    first_len = jnp.where(jnp.arange(N_DP) == fullest, DOC_MAX, pieces[:, 0])
    pieces = pieces.at[:, 0].set(first_len)
    doc_ends = jnp.minimum(jnp.cumsum(pieces, axis=1), totals[:, None])
    earlier = jnp.concatenate([jnp.zeros((N_DP, 1), doc_ends.dtype), doc_ends[:, :-1]], axis=1)
    return (doc_ends - earlier).astype(jnp.int32)


def draw_keys(key, part):
    key = jax.random.fold_in(key, 3)
    return jax.random.truncated_normal(key, -6.0, 6.0, (TOTAL_TOKENS, KEY_VALUE_HEADS * HEAD_DIMENSION)).astype(jnp.bfloat16)


def draw_queries(key, part):
    key = jax.random.fold_in(key, 5)
    return jax.random.truncated_normal(key, -6.0, 6.0, (TOTAL_TOKENS, QUERY_HEADS * HEAD_DIMENSION)).astype(jnp.bfloat16)


def block_scale(own_key, dims, shards, least, high):
    loudness, own = 1.0, jax.random.fold_in(own_key, 6)
    for axis_at, shards_of in shards:
        steps = jnp.exp(jax.random.uniform(jax.random.fold_in(own, axis_at), (shards_of,), jnp.float32, least / len(shards), high / len(shards)))
        loudness = loudness * jnp.repeat(steps, dims[axis_at] // shards_of).reshape([-1 if axis == axis_at else 1 for axis in range(len(dims))])
    return loudness


def scatter_about(rng, extent, deviation, bound, cuts=(), kind=jnp.bfloat16):
    array = jax.random.normal(rng, extent, jnp.float32) * deviation
    if len(cuts) > 0:
        array = block_scale(rng, extent, cuts, -0.22, 0.18) * array
    return jnp.clip(array, min=-bound, max=bound).astype(kind)


def setup_inputs(seed: int = 0) -> dict:
    key_list = jax.random.split(jax.random.key(seed), 6)
    return {
        "queries": draw_queries(jax.random.fold_in(key_list[5], 71), 0),
        "keys": draw_keys(jax.random.fold_in(key_list[5], 71), 0),
        "values": scatter_about(key_list[2], (TOTAL_TOKENS, KEY_VALUE_HEADS * HEAD_DIMENSION), 1.0, 6.0, ((0, 256),)),
        "row_offsets": draw_row_offsets(jax.random.fold_in(key_list[5], 71), 0),
        "doc_lengths": draw_doc_lengths(jax.random.fold_in(key_list[5], 71), 0),
    }


NEG_FILL = -1.0e30


def reference(queries, keys, values, row_offsets, doc_lengths):
    rows_of_group = N_SEQ * ROWS_MAX
    queries_per_key_head = QUERY_HEADS // KEY_VALUE_HEADS
    following = jnp.concatenate([row_offsets[:, 1:], jnp.full((N_DP * N_SEQ, 1), TOK_DEV, jnp.int32)], axis=1)
    counts = (following - row_offsets).astype(jnp.int32)
    owner_dev = (jnp.arange(N_DP, dtype=jnp.int32)[None, :] * N_SEQ + jnp.arange(N_SEQ, dtype=jnp.int32)[:, None]).reshape(-1)
    position = jnp.arange(rows_of_group, dtype=jnp.int32)
    score_scale = HEAD_DIMENSION ** -0.5

    def per_group(group_id):
        seg_sizes = jnp.take(jnp.take(counts, group_id, axis=1), owner_dev)
        seg_starts = jnp.take(jnp.take(row_offsets, group_id, axis=1), owner_dev)
        seg_ends = jnp.cumsum(seg_sizes).astype(jnp.int32)
        segment_id = jnp.minimum(jnp.sum((seg_ends[None, :] <= position[:, None]).astype(jnp.int32), axis=1), N_DP * N_SEQ - 1)
        is_real = position < seg_ends[-1]
        loader_source_row = jnp.take(owner_dev, segment_id) * TOK_DEV + jnp.take(seg_starts, segment_id) + position - jnp.take(seg_ends - seg_sizes, segment_id)
        loader_source_row = jnp.where(is_real, loader_source_row, 0).astype(jnp.int32)
        doc_ends = jnp.cumsum(jnp.take(doc_lengths, group_id, axis=0)).astype(jnp.int32)
        doc_ids = jnp.where(is_real, jnp.sum((doc_ends[None, :] <= position[:, None]).astype(jnp.int32), axis=1), -1)
        allowed = (doc_ids[:, None] == doc_ids[None, :]) & (position[None, :] <= position[:, None]) & is_real[None, :]
        group_queries = jnp.take(queries, loader_source_row, axis=0).astype(jnp.float32).reshape(rows_of_group, KEY_VALUE_HEADS, queries_per_key_head, HEAD_DIMENSION)
        group_keys = jnp.take(keys, loader_source_row, axis=0).astype(jnp.float32).reshape(rows_of_group, KEY_VALUE_HEADS, HEAD_DIMENSION)
        group_values = jnp.take(values, loader_source_row, axis=0).astype(jnp.float32).reshape(rows_of_group, KEY_VALUE_HEADS, HEAD_DIMENSION)

        def each_head_result(kv_head):
            scores = jnp.einsum("qgd,kd->gqk", group_queries[:, kv_head], group_keys[:, kv_head]) * score_scale
            row_top = jnp.max(jnp.where(allowed[None], scores, NEG_FILL), axis=2)
            expo_terms = jnp.where(allowed[None], jnp.exp(scores - row_top[..., None]), 0.0)
            denom = jnp.sum(expo_terms, axis=2)
            rounded_terms = lax.optimization_barrier(expo_terms.astype(jnp.bfloat16)).astype(jnp.float32)
            weighted = jnp.einsum("gqk,kd->qgd", rounded_terms, group_values[:, kv_head])
            denom = jnp.where(denom > 0.0, denom, 1.0)
            return weighted / jnp.transpose(denom)[:, :, None]

        output_per_head = lax.map(each_head_result, jnp.arange(KEY_VALUE_HEADS, dtype=jnp.int32))
        result = jnp.transpose(output_per_head, (1, 0, 2, 3)).reshape(rows_of_group, QUERY_HEADS * HEAD_DIMENSION).astype(jnp.bfloat16)
        return result, jnp.where(is_real, loader_source_row, TOTAL_TOKENS).astype(jnp.int32)

    results, targets = lax.map(per_group, jnp.arange(N_DP, dtype=jnp.int32))
    empty_out = jnp.zeros((TOTAL_TOKENS, QUERY_HEADS * HEAD_DIMENSION), jnp.bfloat16)
    return empty_out.at[targets.reshape(-1)].set(results.reshape(-1, QUERY_HEADS * HEAD_DIMENSION), mode="drop")
```

```python
import functools
import math

import jax
import jax.numpy as jnp
from jax import lax
from jax.experimental import pallas as pl
from jax.experimental.pallas import tpu as pltpu
from jax.sharding import PartitionSpec as P

MESH = pl.DeviceIdType.MESH
HEAD = 128
NEG_FILL = -1e30
BIG = 1 << 30
VMEM_LIMIT = 50 * 1024 * 1024


class Sizes:
    def __init__(self, dp_count, seq_count, tok, width_q, width_k):
        self.groups = dp_count
        self.S = seq_count
        self.Z = width_k // HEAD
        self.X = dp_count // self.Z
        self.tok = tok
        self.slots = 2 * tok // dp_count
        self.seg = 3 * tok // 2
        self.G = width_q // width_k
        self.qw = self.G * HEAD
        self.W = self.qw + 2 * HEAD
        self.flat = self.groups * self.slots
        self.per_s = self.X * self.Z * self.slots
        self.rows = self.S * self.seg
        self.blk = math.gcd(self.rows, 256)
        self.nb = self.rows // self.blk


def near_first(count):
    order = [0]
    for dist in range(1, count // 2 + 1):
        order.append(dist)
        if count - dist != dist:
            order.append(count - dist)
    return order


def greet(n, x, z, s):
    barrier = pltpu.get_barrier_semaphore()
    plane = x * n.S + s
    count = n.X * n.S

    def one_plane(t, carry):
        p = lax.rem(plane + t, count)
        pl.semaphore_signal(
            barrier, inc=1, device_id=((p // n.S) * n.Z + z, lax.rem(p, n.S)), device_id_type=MESH
        )
        return carry

    lax.fori_loop(1, count, one_plane, 0)

    def one_line(t, carry):
        zt = lax.rem(z + t, n.Z)
        pl.semaphore_signal(barrier, inc=1, device_id=(x * n.Z + zt, s), device_id_type=MESH)
        return carry

    lax.fori_loop(1, n.Z, one_line, 0)
    pl.semaphore_wait(barrier, count - 1 + n.Z - 1)


def in_kernel(n, q_ref, k_ref, v_ref, idx_ref, out_ref, zbuf, sbuf, zsend, zrecv, psend, precv, own_sem):
    dp, s = lax.axis_index("dp"), lax.axis_index("seq")
    x, z = dp // n.Z, lax.rem(dp, n.Z)
    plane = x * n.S + s
    count = n.X * n.S
    mine = s * n.X + x
    qw = n.qw
    order = near_first(n.Z)

    def parts(zt, delta):
        return (
            (q_ref.at[:, pl.ds(pl.multiple_of(zt * qw, qw), qw)], zbuf.at[delta, :, pl.ds(0, qw)]),
            (k_ref.at[:, pl.ds(pl.multiple_of(zt * HEAD, HEAD), HEAD)], zbuf.at[delta, :, pl.ds(qw, HEAD)]),
            (v_ref.at[:, pl.ds(pl.multiple_of(zt * HEAD, HEAD), HEAD)], zbuf.at[delta, :, pl.ds(qw + HEAD, HEAD)]),
        )

    for src, dst in parts(z, 0):
        pltpu.make_async_copy(src, dst, zrecv.at[0]).start()
    greet(n, x, z, s)
    for delta in order[1:]:
        zt = lax.rem(z + delta, n.Z)
        for src, dst in parts(zt, delta):
            pltpu.make_async_remote_copy(
                src_ref=src,
                dst_ref=dst,
                send_sem=zsend.at[delta],
                recv_sem=zrecv.at[delta],
                device_id=(x * n.Z + zt, s),
                device_id_type=MESH,
            ).start()

    lane = lax.broadcasted_iota(jnp.int32, (n.flat, n.tok), 1)
    for step, delta in enumerate(order):
        pltpu.make_async_copy(zbuf.at[delta], zbuf.at[delta], zrecv.at[delta]).wait()
        pick = (lane == idx_ref[:, step : step + 1]).astype(jnp.bfloat16)
        padded = jnp.dot(pick, zbuf[delta], preferred_element_type=jnp.float32).astype(jnp.bfloat16)
        sbuf[delta] = padded.reshape(n.groups, n.slots, n.W)
        z_src = lax.rem(z - delta + n.Z, n.Z)
        pltpu.make_async_copy(sbuf.at[delta, plane], out_ref.at[mine, z_src], own_sem).start()

        def send(t, carry):
            p = lax.rem(plane + t, count)
            pltpu.make_async_remote_copy(
                src_ref=sbuf.at[delta, p],
                dst_ref=out_ref.at[mine, z_src],
                send_sem=psend.at[t],
                recv_sem=precv.at[mine],
                device_id=((p // n.S) * n.Z + z, lax.rem(p, n.S)),
                device_id_type=MESH,
            ).start()
            return carry

        lax.fori_loop(1, count, send, 0)

    pltpu.make_async_copy(out_ref.at[mine], out_ref.at[mine], own_sem).wait()

    def finish(t, carry):
        p = lax.rem(plane + t, count)
        src = lax.rem(p, n.S) * n.X + p // n.S
        pltpu.make_async_copy(out_ref.at[src], out_ref.at[src], precv.at[src]).wait()
        pltpu.make_async_copy(out_ref.at[src], out_ref.at[src], psend.at[t]).wait()
        return carry

    lax.fori_loop(1, count, finish, 0)
    for delta in order[1:]:
        pltpu.make_async_copy(zbuf.at[delta], zbuf.at[delta], zsend.at[delta]).wait()


def route_in(n, q, k, v, idx_cols):
    anyspace = pl.BlockSpec(memory_space=pl.ANY)
    return pl.pallas_call(
        functools.partial(in_kernel, n),
        out_shape=jax.ShapeDtypeStruct((n.S * n.X, n.Z, n.slots, n.W), jnp.bfloat16),
        in_specs=[anyspace, anyspace, anyspace, pl.BlockSpec(memory_space=pltpu.VMEM)],
        out_specs=anyspace,
        scratch_shapes=[
            pltpu.VMEM((n.Z, n.tok, n.W), jnp.bfloat16),
            pltpu.VMEM((n.Z, n.groups, n.slots, n.W), jnp.bfloat16),
            pltpu.SemaphoreType.DMA((n.Z,)),
            pltpu.SemaphoreType.DMA((n.Z,)),
            pltpu.SemaphoreType.DMA((n.X * n.S,)),
            pltpu.SemaphoreType.DMA((n.X * n.S,)),
            pltpu.SemaphoreType.DMA,
        ],
        compiler_params=pltpu.CompilerParams(
            collective_id=0, has_side_effects=True, vmem_limit_bytes=VMEM_LIMIT
        ),
        name="route_in",
    )(q, k, v, idx_cols)


def attend_kernel(n, base_ref, tot_ref, low_ref, last_ref, rows_ref, dst_ref, ends_ref, out_ref,
                  rbuf, comp, strip, top, total, acc, sems):
    copies = [pltpu.make_async_copy(rows_ref.at[s], rbuf.at[s], sems.at[s]) for s in range(n.S)]
    for c in copies:
        c.start()
    sub = lax.broadcasted_iota(jnp.int32, (n.seg, n.per_s), 0)
    for s in range(n.S):
        copies[s].wait()
        pick = (sub == dst_ref[s : s + 1, :]).astype(jnp.bfloat16)
        comp[s * n.seg : (s + 1) * n.seg, :] = jnp.dot(
            pick, rbuf[s], preferred_element_type=jnp.float32
        ).astype(jnp.bfloat16)

    blk, qw = n.blk, n.qw
    half = min(128, blk)
    gain = HEAD ** -0.5 * math.log2(math.e)

    def positions(b, shape, dim, missing):
        u = lax.broadcasted_iota(jnp.int32, shape, dim) + b * blk
        s1 = (b * blk) // n.seg
        s2 = jnp.minimum(s1 + 1, n.S - 1)
        r1 = u - s1 * n.seg
        r2 = r1 - n.seg
        first = jnp.where(r1 < tot_ref[s1], base_ref[s1] + r1, missing)
        second = jnp.where(r2 < tot_ref[s2], base_ref[s2] + r2, missing)
        return jnp.where(r1 < n.seg, first, second)

    def q_block(i, carry):
        start = pl.multiple_of(i * blk, blk)

        @pl.when(last_ref[i] < 0)
        def _():
            out_ref[pl.ds(start, blk), :] = jnp.zeros((blk, qw), out_ref.dtype)

        @pl.when(last_ref[i] >= 0)
        def _():
            q_pos = positions(i, (blk, 1), 0, -1)
            ends = ends_ref[...]
            q_low = jnp.max(jnp.where(ends <= q_pos, ends, 0), axis=1, keepdims=True)
            top[...] = jnp.full(top.shape, NEG_FILL, jnp.float32)
            total[...] = jnp.zeros(total.shape, jnp.float32)
            acc[...] = jnp.zeros(acc.shape, jnp.float32)
            low = low_ref[i]

            def scores(b, carry):
                @pl.when(last_ref[b] >= low)
                def _():
                    k_pos = positions(b, (1, blk), 1, BIG)
                    allowed = (k_pos >= q_low) & (k_pos <= q_pos)
                    k_start = pl.multiple_of(b * blk, blk)
                    keys = comp[pl.ds(k_start, blk), qw : qw + HEAD]
                    for h in range(n.G):
                        sc = lax.dot_general(
                            comp[pl.ds(start, blk), h * HEAD : (h + 1) * HEAD],
                            keys,
                            (((1,), (1,)), ((), ())),
                            preferred_element_type=jnp.float32,
                        )
                        sc = jnp.where(allowed, sc, NEG_FILL)
                        strip[b, h] = sc
                        best = top[h]
                        for c in range(0, blk, half):
                            best = jnp.maximum(best, sc[:, c : c + half])
                        top[h] = best

                return carry

            lax.fori_loop(0, i + 1, scores, 0)
            for h in range(n.G):
                row = jnp.max(top[h], axis=1, keepdims=True) * gain
                top[h] = jnp.broadcast_to(row, (blk, half))

            def weigh(b, carry):
                @pl.when(last_ref[b] >= low)
                def _():
                    k_start = pl.multiple_of(b * blk, blk)
                    vals = comp[pl.ds(k_start, blk), qw + HEAD : qw + 2 * HEAD]
                    for h in range(n.G):
                        w = jnp.exp2(strip[b, h] * gain - top[h][:, 0:1])
                        sums = total[h]
                        for c in range(0, blk, half):
                            sums = sums + w[:, c : c + half]
                        total[h] = sums
                        acc[h] += jnp.dot(w.astype(jnp.bfloat16), vals, preferred_element_type=jnp.float32)

                return carry

            lax.fori_loop(0, i + 1, weigh, 0)
            for h in range(n.G):
                denom = jnp.sum(total[h], axis=1, keepdims=True)
                denom = jnp.where(denom > 0.0, denom, 1.0)
                out_ref[pl.ds(start, blk), h * HEAD : (h + 1) * HEAD] = (acc[h] / denom).astype(out_ref.dtype)

        return carry

    lax.fori_loop(0, n.nb, q_block, 0)


def attend(n, rows, dst, base, tot, low, last, ends):
    smem = pl.BlockSpec(memory_space=pltpu.SMEM)
    vmem = pl.BlockSpec(memory_space=pltpu.VMEM)
    half = min(128, n.blk)
    return pl.pallas_call(
        functools.partial(attend_kernel, n),
        out_shape=jax.ShapeDtypeStruct((n.rows, n.qw), jnp.bfloat16),
        in_specs=[smem, smem, smem, smem, pl.BlockSpec(memory_space=pl.ANY), vmem, vmem],
        out_specs=vmem,
        scratch_shapes=[
            pltpu.VMEM((n.S, n.per_s, n.W), jnp.bfloat16),
            pltpu.VMEM((n.rows, n.W), jnp.bfloat16),
            pltpu.VMEM((n.nb, n.G, n.blk, n.blk), jnp.float32),
            pltpu.VMEM((n.G, n.blk, half), jnp.float32),
            pltpu.VMEM((n.G, n.blk, half), jnp.float32),
            pltpu.VMEM((n.G, n.blk, HEAD), jnp.float32),
            pltpu.SemaphoreType.DMA((n.S,)),
        ],
        compiler_params=pltpu.CompilerParams(vmem_limit_bytes=VMEM_LIMIT),
        name="attend",
    )(base, tot, low, last, rows, dst, ends)


def out_kernel(n, att_ref, dst_ref, idx_ref, out_ref, ubuf, rbuf, fbuf, usend, urecv, fsend, frecv):
    dp, s = lax.axis_index("dp"), lax.axis_index("seq")
    x, z = dp // n.Z, lax.rem(dp, n.Z)
    plane = x * n.S + s
    count = n.X * n.S
    qw = n.qw
    order = near_first(n.Z)[::-1]

    lane = lax.broadcasted_iota(jnp.int32, (n.per_s, n.seg), 1)
    for part in range(n.S):
        pick = (lane == dst_ref[:, part : part + 1]).astype(jnp.bfloat16)
        spread = jnp.dot(
            pick, att_ref[part * n.seg : (part + 1) * n.seg, :], preferred_element_type=jnp.float32
        ).astype(jnp.bfloat16)
        ubuf[part] = spread.reshape(n.X, n.Z, n.slots, qw)
    greet(n, x, z, s)

    for delta in order:
        zt = lax.rem(z + delta, n.Z)
        pltpu.make_async_copy(ubuf.at[s, x, zt], rbuf.at[delta, plane], urecv.at[delta]).start()

        def send(t, carry):
            p = lax.rem(plane + t, count)
            pltpu.make_async_remote_copy(
                src_ref=ubuf.at[lax.rem(p, n.S), p // n.S, zt],
                dst_ref=rbuf.at[delta, plane],
                send_sem=usend.at[delta],
                recv_sem=urecv.at[delta],
                device_id=((p // n.S) * n.Z + z, lax.rem(p, n.S)),
                device_id_type=MESH,
            ).start()
            return carry

        lax.fori_loop(1, count, send, 0)

    sub = lax.broadcasted_iota(jnp.int32, (n.tok, n.flat), 0)
    columns = pl.ds(pl.multiple_of(z * qw, qw), qw)
    for step, delta in enumerate(order):
        zt = lax.rem(z + delta, n.Z)
        pltpu.make_async_copy(rbuf.at[delta], rbuf.at[delta], urecv.at[delta]).wait()
        pick = (sub == idx_ref[step : step + 1, :]).astype(jnp.bfloat16)
        fbuf[delta] = jnp.dot(
            pick, rbuf[delta].reshape(n.flat, qw), preferred_element_type=jnp.float32
        ).astype(jnp.bfloat16)
        if delta == 0:
            pltpu.make_async_copy(fbuf.at[0], out_ref.at[:, columns], frecv.at[0]).start()
        else:
            pltpu.make_async_remote_copy(
                src_ref=fbuf.at[delta],
                dst_ref=out_ref.at[:, columns],
                send_sem=fsend.at[delta],
                recv_sem=frecv.at[delta],
                device_id=(x * n.Z + zt, s),
                device_id_type=MESH,
            ).start()

    for delta in order:
        pltpu.make_async_copy(fbuf.at[delta], fbuf.at[delta], frecv.at[delta]).wait()
        if delta != 0:
            pltpu.make_async_copy(fbuf.at[delta], fbuf.at[delta], fsend.at[delta]).wait()
        some = rbuf.at[delta, pl.ds(0, count - 1)]
        pltpu.make_async_copy(some, some, usend.at[delta]).wait()


def route_out(n, att, dst_cols, idx):
    vmem = pl.BlockSpec(memory_space=pltpu.VMEM)
    return pl.pallas_call(
        functools.partial(out_kernel, n),
        out_shape=jax.ShapeDtypeStruct((n.tok, n.Z * n.qw), jnp.bfloat16),
        in_specs=[vmem, vmem, vmem],
        out_specs=pl.BlockSpec(memory_space=pl.ANY),
        scratch_shapes=[
            pltpu.VMEM((n.S, n.X, n.Z, n.slots, n.qw), jnp.bfloat16),
            pltpu.VMEM((n.Z, n.groups, n.slots, n.qw), jnp.bfloat16),
            pltpu.VMEM((n.Z, n.tok, n.qw), jnp.bfloat16),
            pltpu.SemaphoreType.DMA((n.Z,)),
            pltpu.SemaphoreType.DMA((n.Z,)),
            pltpu.SemaphoreType.DMA((n.Z,)),
            pltpu.SemaphoreType.DMA((n.Z,)),
        ],
        compiler_params=pltpu.CompilerParams(
            collective_id=1, has_side_effects=True, vmem_limit_bytes=VMEM_LIMIT
        ),
        name="route_out",
    )(att, dst_cols, idx)


def on_device(queries, keys, values, row_offsets, doc_lengths):
    n = Sizes(lax.axis_size("dp"), lax.axis_size("seq"), queries.shape[0], queries.shape[1], keys.shape[1])
    dp, s = lax.axis_index("dp"), lax.axis_index("seq")
    x, z = dp // n.Z, lax.rem(dp, n.Z)
    group = x * n.S + s
    row_ends = jnp.concatenate(
        [row_offsets[:, 1:], jnp.full((row_offsets.shape[0], 1), n.tok, jnp.int32)], axis=1
    )
    counts = row_ends - row_offsets
    slot = jnp.arange(n.slots, dtype=jnp.int32)

    def line(table):
        grid = table.reshape(n.X, n.Z, n.S, n.groups)
        return lax.dynamic_slice(grid, (x, 0, s, 0), (1, n.Z, 1, n.groups)).reshape(n.Z, n.groups)

    line_starts, line_counts = line(row_offsets), line(counts)
    idx = jnp.where(
        slot[None, None, :] < line_counts[:, :, None], line_starts[:, :, None] + slot[None, None, :], -1
    ).reshape(n.Z, n.flat)
    near = jnp.asarray(near_first(n.Z), jnp.int32)
    idx_in = jnp.transpose(jnp.take(idx, lax.rem(z - near + n.Z, n.Z), axis=0))
    idx_out = jnp.take(idx, lax.rem(z + near[::-1], n.Z), axis=0)

    column = lax.dynamic_index_in_dim(counts, group, 1, keepdims=False)
    count_grid = jnp.transpose(column.reshape(n.groups, n.S))
    tot = jnp.sum(count_grid, axis=1)
    base = jnp.cumsum(tot) - tot
    dp_base = jnp.cumsum(count_grid, axis=1) - count_grid
    dst = jnp.where(
        slot[None, None, :] < count_grid[:, :, None], dp_base[:, :, None] + slot[None, None, :], -1
    ).reshape(n.S, n.per_s)
    ends = jnp.cumsum(lax.dynamic_index_in_dim(doc_lengths, group, 0, keepdims=False))

    u = jnp.arange(n.rows, dtype=jnp.int32).reshape(n.S, n.seg)
    r = u - u[:, :1]
    pos = jnp.where(r < tot[:, None], base[:, None] + r, -1).reshape(n.nb, n.blk)
    last = jnp.max(pos, axis=1)
    first = jnp.min(jnp.where(pos >= 0, pos, BIG), axis=1)
    low = jnp.max(jnp.where(ends[None, :] <= first[:, None], ends[None, :], 0), axis=1)

    rows = route_in(n, queries, keys, values, idx_in)
    att = attend(
        n, rows.reshape(n.S, n.per_s, n.W), dst, base, tot, low, last, ends.reshape(1, -1)
    )
    return route_out(n, att, jnp.transpose(dst), idx_out)


def solution(mesh):
    return jax.shard_map(
        on_device,
        mesh=mesh,
        in_specs=(P(("dp", "seq"), None), P(("dp", "seq"), None), P(("dp", "seq"), None), P(), P()),
        out_specs=P(("dp", "seq"), None),
        check_vma=False,
    )
```

```python
import functools
import math

import jax
import jax.numpy as jnp
from jax import lax
from jax.experimental import pallas as pl
from jax.experimental.pallas import tpu as pltpu
from jax.sharding import PartitionSpec as P

MESH = pl.DeviceIdType.MESH
HEAD = 128
NEG_FILL = -1e30
BIG = 1 << 30
VMEM_LIMIT = 54 * 1024 * 1024


class Sizes:
    def __init__(self, dp_count, seq_count, tok, width_q, width_k, groups):
        self.groups = groups
        self.S = seq_count
        self.Z = width_k // HEAD
        self.X = dp_count // self.Z
        self.tok = tok
        self.slots = 2 * tok // groups
        self.seg = 3 * dp_count * tok // (2 * groups)
        self.G = width_q // width_k
        self.qw = self.G * HEAD
        self.nh = self.G // 2
        self.hw = self.nh * HEAD
        self.widths = (self.hw + 2 * HEAD, self.hw)
        self.flat = self.groups * self.slots
        self.per_s = self.X * self.Z * self.slots
        self.rows = self.S * self.seg
        self.blk = 2 * self.seg // 3
        self.nb = self.rows // self.blk
        self.pad = 3 * self.blk
        self.wide = 4 * self.blk
        order = [0]
        runs = [(0, 1)]
        for dist in range(1, self.Z // 2 + 1):
            at = len(order)
            order.append(dist)
            if self.Z - dist != dist:
                order.append(self.Z - dist)
            runs.append((at, len(order)))
        self.order = order
        self.runs = runs


def greet(n, x, z, s):
    barrier = pltpu.get_barrier_semaphore()
    plane = x * n.S + s
    count = n.X * n.S

    def one_plane(t, carry):
        p = lax.rem(plane + t, count)
        pl.semaphore_signal(
            barrier, inc=1, device_id=((p // n.S) * n.Z + z, lax.rem(p, n.S)), device_id_type=MESH
        )
        return carry

    lax.fori_loop(1, count, one_plane, 0)

    def one_line(t, carry):
        zt = lax.rem(z + t, n.Z)
        pl.semaphore_signal(barrier, inc=1, device_id=(x * n.Z + zt, s), device_id_type=MESH)
        return carry

    lax.fori_loop(1, n.Z, one_line, 0)
    pl.semaphore_wait(barrier, count - 1 + n.Z - 1)


def fused_kernel(n, base_ref, tot_ref, q_ref, k_ref, v_ref, idx_cols, idx_rows, dst_cols, dst_rows, ends_ref, kpos_ref,
                 out_ref, zb0, zb1, sb0, sb1, rc0, rc1, qbuf, kbuf, vbuf, strip, top, acc, qpos, qlow, obuf, ub, rb, fb,
                 zsend, zrecv, psend, precv, usend, urecv, fsend, frecv):
    dp, s = lax.axis_index("dp"), lax.axis_index("seq")
    x, z = dp // n.Z, lax.rem(dp, n.Z)
    plane = x * n.S + s
    count = n.X * n.S
    mine = s * n.X + x
    blk, hw, wide = n.blk, n.hw, n.wide
    half = min(128, blk)
    gain = HEAD ** -0.5 * math.log2(math.e)
    zb, sb, rc = (zb0, zb1), (sb0, sb1), (rc0, rc1)

    def done(ref, sem):
        pltpu.make_async_copy(ref, ref, sem).wait()

    def remote(src, dst, send, recv, dp_to, s_to):
        pltpu.make_async_remote_copy(
            src_ref=src, dst_ref=dst, send_sem=send, recv_sem=recv,
            device_id=(dp_to, s_to), device_id_type=MESH,
        ).start()

    def to_plane(body):
        def one(t, carry):
            p = lax.rem(plane + t, count)
            body(p // n.S, lax.rem(p, n.S))
            return carry

        lax.fori_loop(1, count, one, 0)

    def z_of(place):
        return lax.rem(z - n.order[place] + n.Z, n.Z)

    def parts(piece, zt, place):
        first = pl.multiple_of(zt * n.qw + piece * hw, hw)
        found = [(q_ref.at[:, pl.ds(first, hw)], zb[piece].at[place, :, pl.ds(0, hw)])]
        if piece == 0:
            cols = pl.ds(pl.multiple_of(zt * HEAD, HEAD), HEAD)
            found.append((k_ref.at[:, cols], zb0.at[place, :, pl.ds(hw, HEAD)]))
            found.append((v_ref.at[:, cols], zb0.at[place, :, pl.ds(hw + HEAD, HEAD)]))
        return found

    def z_start(piece, place):
        if place == 0:
            for src, dst in parts(piece, z, 0):
                pltpu.make_async_copy(src, dst, zrecv.at[piece, 0]).start()
            return
        zt = lax.rem(z + n.order[place], n.Z)
        for src, dst in parts(piece, zt, place):
            remote(src, dst, zsend.at[piece, place], zrecv.at[piece, place], x * n.Z + zt, s)

    lane = lax.broadcasted_iota(jnp.int32, (n.flat, n.tok), 1)

    def in_run(piece, run, after=None):
        first, last = n.runs[run]
        for place in range(first, last):
            done(zb[piece].at[place], zrecv.at[piece, place])
            if after is not None:
                after(place)
            pick = (lane == idx_cols[:, place : place + 1]).astype(jnp.bfloat16)
            padded = jnp.dot(pick, zb[piece][place], preferred_element_type=jnp.float32).astype(jnp.bfloat16)
            sb[piece][:, place] = padded.reshape(n.groups, n.slots, n.widths[piece])
        run_of = pl.ds(first, last - first)
        pltpu.make_async_copy(sb[piece].at[plane, run_of], rc[piece].at[mine, run_of], precv.at[piece]).start()
        to_plane(
            lambda xt, st: remote(
                sb[piece].at[xt * n.S + st, run_of], rc[piece].at[mine, run_of],
                psend.at[piece, run], precv.at[piece], xt * n.Z + z, st,
            )
        )

    def compact(piece):
        done(rc[piece], precv.at[piece])
        sub = lax.broadcasted_iota(jnp.int32, (n.seg, n.per_s), 0)
        for k in range(n.S):
            pick = (sub == dst_rows[k : k + 1, :]).astype(jnp.bfloat16)
            block = rc[piece][k * n.X : (k + 1) * n.X].reshape(n.per_s, n.widths[piece])
            comp = jnp.dot(pick, block, preferred_element_type=jnp.float32).astype(jnp.bfloat16)
            for h in range(n.nh):
                qbuf[piece, h, k * n.seg : (k + 1) * n.seg, :] = comp[:, h * HEAD : (h + 1) * HEAD]
            if piece == 0:
                at = n.pad + k * n.seg
                kbuf[at : at + n.seg, :] = comp[:, hw : hw + HEAD]
                vbuf[at : at + n.seg, 0:HEAD] = comp[:, hw + HEAD :]

    def query_places(i, carry):
        start = pl.multiple_of(i * blk, blk)
        u = lax.broadcasted_iota(jnp.int32, (blk, 1), 0) + start
        s1 = start // n.seg
        s2 = jnp.minimum(s1 + 1, n.S - 1)
        r1 = u - s1 * n.seg
        r2 = r1 - n.seg
        one = jnp.where(r1 < tot_ref[s1], base_ref[s1] + r1, -1)
        two = jnp.where(r2 < tot_ref[s2], base_ref[s2] + r2, -1)
        pos = jnp.where(r1 < n.seg, one, two)
        ends = ends_ref[...]
        low = jnp.max(jnp.where(ends <= pos, ends, 0), axis=1, keepdims=True)
        qpos[pl.ds(start, blk), :] = jnp.broadcast_to(pos, (blk, half))
        qlow[pl.ds(start, blk), :] = jnp.broadcast_to(low, (blk, half))
        return carry

    def attend(piece, i):
        start = pl.multiple_of(i * blk, blk)
        top[...] = jnp.full(top.shape, NEG_FILL, jnp.float32)
        acc[...] = jnp.zeros(acc.shape, jnp.float32)
        chunks = (i + 4) // 4

        def at_keys(j):
            return pl.multiple_of((i + 1) * blk - wide * (j + 1) + n.pad, blk)

        def scores(j, carry):
            queries = qbuf[piece, :, pl.ds(start, blk), :].reshape(n.nh * blk, HEAD)
            sc = lax.dot_general(
                queries, kbuf[pl.ds(at_keys(j), wide), :],
                (((1,), (1,)), ((), ())), preferred_element_type=jnp.float32,
            )
            high, low = qpos[pl.ds(start, blk), :], qlow[pl.ds(start, blk), :]
            k_pos = kpos_ref[:, pl.ds(at_keys(j), wide)]
            best = top[...]
            for col in range(0, wide, half):
                here = k_pos[:, col : col + half]
                allowed = (here >= low) & (here <= high)
                part = jnp.where(
                    allowed[None], sc[:, col : col + half].reshape(n.nh, blk, half), NEG_FILL
                ).reshape(n.nh * blk, half)
                strip[j, :, col : col + half] = part
                best = jnp.maximum(best, part)
            top[...] = best
            return carry

        lax.fori_loop(0, chunks, scores, 0)
        top[...] = jnp.broadcast_to(jnp.max(top[...], axis=1, keepdims=True) * gain, top.shape)

        def weigh(j, carry):
            row = top[...]
            pieces = [
                jnp.exp2(strip[j, :, col : col + half] * gain - row).astype(jnp.bfloat16)
                for col in range(0, wide, half)
            ]
            acc[...] += jnp.dot(
                jnp.concatenate(pieces, axis=1), vbuf[pl.ds(at_keys(j), wide), :],
                preferred_element_type=jnp.float32,
            )
            return carry

        lax.fori_loop(0, chunks, weigh, 0)
        denom = acc[:, HEAD:]
        result = (acc[:, :HEAD] / jnp.where(denom > 0.0, denom, 1.0)).astype(obuf.dtype)
        for h in range(n.nh):
            obuf[pl.ds(start, blk), h * HEAD : (h + 1) * HEAD] = result[h * blk : (h + 1) * blk]

    def out_all(piece):
        wide_lane = lax.broadcasted_iota(jnp.int32, (n.per_s, n.seg), 1)
        for k in range(n.S):
            pick = (wide_lane == dst_cols[:, k : k + 1]).astype(jnp.bfloat16)
            spread = jnp.dot(
                pick, obuf[k * n.seg : (k + 1) * n.seg, :], preferred_element_type=jnp.float32
            ).astype(jnp.bfloat16)
            ub[piece, k] = spread.reshape(n.X, n.Z, n.slots, hw)
        for run in reversed(range(len(n.runs))):
            first, last = n.runs[run]
            run_of = pl.ds(first, last - first)
            pltpu.make_async_copy(
                ub.at[piece, s, x, run_of], rb.at[piece, plane, run_of], urecv.at[piece, run]
            ).start()
            to_plane(
                lambda xt, st: remote(
                    ub.at[piece, st, xt, run_of], rb.at[piece, plane, run_of],
                    usend.at[piece, run], urecv.at[piece, run], xt * n.Z + z, st,
                )
            )

    tall = lax.broadcasted_iota(jnp.int32, (n.tok, n.flat), 0)

    def hand_back(piece, run):
        first, last = n.runs[run]
        done(rb.at[piece, :, pl.ds(first, last - first)], urecv.at[piece, run])
        cols = pl.ds(pl.multiple_of(z * n.qw + piece * hw, hw), hw)
        for place in range(first, last):
            pick = (tall == idx_rows[place : place + 1, :]).astype(jnp.bfloat16)
            fb[piece, place] = jnp.dot(
                pick, rb[piece, :, place].reshape(n.flat, hw), preferred_element_type=jnp.float32
            ).astype(jnp.bfloat16)
            if place == 0:
                pltpu.make_async_copy(fb.at[piece, 0], out_ref.at[:, cols], frecv.at[piece, 0]).start()
            else:
                remote(
                    fb.at[piece, place], out_ref.at[:, cols],
                    fsend.at[piece, place], frecv.at[piece, place], x * n.Z + z_of(place), s,
                )

    places = range(n.Z)
    runs = len(n.runs)
    z_start(0, 0)
    z_start(1, 0)
    greet(n, x, z, s)
    for place in places[1:]:
        z_start(0, place)
    lax.fori_loop(0, n.nb, query_places, 0)
    kbuf[0 : n.pad, :] = jnp.zeros((n.pad, HEAD), kbuf.dtype)
    vbuf[:, 0:HEAD] = jnp.zeros((n.rows + n.pad, HEAD), vbuf.dtype)
    vbuf[:, HEAD:] = jnp.ones((n.rows + n.pad, HEAD), vbuf.dtype)

    def then_second(place):
        if place:
            z_start(1, place)

    for run in range(runs - 1):
        in_run(0, run, then_second)
    in_run(1, 0)
    in_run(0, runs - 1, then_second)
    compact(0)

    def block(t, carry):
        @pl.when(t == n.nb)
        def _():
            out_all(0)
            compact(1)

        piece = t // n.nb
        attend(piece, lax.rem(t, n.nb))
        for run in range(1, runs):

            @pl.when(t == 2 * (run - 1))
            def _(run=run):
                in_run(1, run)

        for k in range(3):

            @pl.when(t == n.nb + 3 + 3 * k)
            def _(k=k):
                if k < runs:
                    hand_back(0, runs - 1 - k)

        return carry

    lax.fori_loop(0, 2 * n.nb, block, 0)
    out_all(1)
    for run in reversed(range(max(runs - 3, 0))):
        hand_back(0, run)
    for run in reversed(range(runs)):
        hand_back(1, run)

    for piece in range(2):
        for place in places:
            done(fb.at[piece, place], frecv.at[piece, place])
            if place:
                done(fb.at[piece, place], fsend.at[piece, place])
                done(zb[piece].at[place], zsend.at[piece, place])
        for run, (first, last) in enumerate(n.runs):
            some = pl.ds(0, count - 1), pl.ds(first, last - first)
            done(sb[piece].at[some], psend.at[piece, run])
            done(rb.at[(piece,) + some], usend.at[piece, run])


def fused(n, q, k, v, idx, dst, base, tot, ends, kpos):
    smem = pl.BlockSpec(memory_space=pltpu.SMEM)
    vmem = pl.BlockSpec(memory_space=pltpu.VMEM)
    anyspace = pl.BlockSpec(memory_space=pl.ANY)
    half = min(128, n.blk)
    w0, w1 = n.widths
    chunks = (n.nb + 3) // 4
    bf, f32 = jnp.bfloat16, jnp.float32
    sem = pltpu.SemaphoreType.DMA
    runs = len(n.runs)
    senders = n.X * n.S
    return pl.pallas_call(
        functools.partial(fused_kernel, n),
        out_shape=jax.ShapeDtypeStruct((n.tok, n.Z * n.qw), bf),
        in_specs=[smem, smem, anyspace, anyspace, anyspace] + [vmem] * 6,
        out_specs=anyspace,
        scratch_shapes=[
            pltpu.VMEM((n.Z, n.tok, w0), bf),
            pltpu.VMEM((n.Z, n.tok, w1), bf),
            pltpu.VMEM((n.groups, n.Z, n.slots, w0), bf),
            pltpu.VMEM((n.groups, n.Z, n.slots, w1), bf),
            pltpu.VMEM((senders, n.Z, n.slots, w0), bf),
            pltpu.VMEM((senders, n.Z, n.slots, w1), bf),
            pltpu.VMEM((2, n.nh, n.rows, HEAD), bf),
            pltpu.VMEM((n.rows + n.pad, HEAD), bf),
            pltpu.VMEM((n.rows + n.pad, 2 * HEAD), bf),
            pltpu.VMEM((chunks, n.nh * n.blk, n.wide), f32),
            pltpu.VMEM((n.nh * n.blk, half), f32),
            pltpu.VMEM((n.nh * n.blk, 2 * HEAD), f32),
            pltpu.VMEM((n.rows, half), jnp.int32),
            pltpu.VMEM((n.rows, half), jnp.int32),
            pltpu.VMEM((n.rows, n.hw), bf),
            pltpu.VMEM((2, n.S, n.X, n.Z, n.slots, n.hw), bf),
            pltpu.VMEM((2, n.groups, n.Z, n.slots, n.hw), bf),
            pltpu.VMEM((2, n.Z, n.tok, n.hw), bf),
            sem((2, n.Z)),
            sem((2, n.Z)),
            sem((2, runs)),
            sem((2,)),
            sem((2, runs)),
            sem((2, runs)),
            sem((2, n.Z)),
            sem((2, n.Z)),
        ],
        compiler_params=pltpu.CompilerParams(
            collective_id=0, has_side_effects=True, vmem_limit_bytes=VMEM_LIMIT
        ),
        name="route_and_attend",
    )(base, tot, q, k, v, jnp.transpose(idx), idx, jnp.transpose(dst), dst, ends, kpos)


def on_device(queries, keys, values, row_offsets, doc_lengths):
    n = Sizes(
        lax.axis_size("dp"), lax.axis_size("seq"), queries.shape[0], queries.shape[1], keys.shape[1],
        row_offsets.shape[1],
    )
    dp, s = lax.axis_index("dp"), lax.axis_index("seq")
    x, z = dp // n.Z, lax.rem(dp, n.Z)
    group = x * n.S + s
    row_ends = jnp.concatenate(
        [row_offsets[:, 1:], jnp.full((row_offsets.shape[0], 1), n.tok, jnp.int32)], axis=1
    )
    counts = row_ends - row_offsets
    slot = jnp.arange(n.slots, dtype=jnp.int32)
    at_z = lax.rem(z - jnp.asarray(n.order, jnp.int32) + n.Z, n.Z)

    loader = (x * n.Z + at_z) * n.S + s
    line_starts = jnp.take(row_offsets, loader, axis=0)
    line_counts = jnp.take(counts, loader, axis=0)
    idx = jnp.where(
        slot[None, None, :] < line_counts[:, :, None], line_starts[:, :, None] + slot[None, None, :], -1
    ).reshape(n.Z, n.flat)

    column = lax.dynamic_index_in_dim(counts, group, 1, keepdims=False)
    count_grid = jnp.transpose(column.reshape(n.X * n.Z, n.S))
    tot = jnp.sum(count_grid, axis=1)
    base = jnp.cumsum(tot) - tot
    dp_base = jnp.cumsum(count_grid, axis=1) - count_grid

    def near(table):
        return jnp.take(table.reshape(n.S, n.X, n.Z), at_z, axis=2)[..., None]

    dst = jnp.where(slot < near(count_grid), near(dp_base) + slot, -1).reshape(n.S, n.per_s)
    ends = jnp.cumsum(lax.dynamic_index_in_dim(doc_lengths, group, 0, keepdims=False)).reshape(1, -1)

    r = jnp.arange(n.seg, dtype=jnp.int32)[None, :]
    kpos = jnp.where(r < tot[:, None], base[:, None] + r, BIG).reshape(1, n.rows)
    kpos = jnp.pad(kpos, ((0, 0), (n.pad, 0)), constant_values=BIG)
    return fused(n, queries, keys, values, idx, dst, base, tot, ends, kpos)


def solution(mesh):
    return jax.shard_map(
        on_device,
        mesh=mesh,
        in_specs=(P(("dp", "seq"), None), P(("dp", "seq"), None), P(("dp", "seq"), None), P(), P()),
        out_specs=P(("dp", "seq"), None),
        check_vma=False,
    )
```

```python
import functools
import math

import jax
import jax.numpy as jnp
from jax import lax
from jax.experimental import pallas as pl
from jax.experimental.pallas import tpu as pltpu
from jax.sharding import PartitionSpec as P

MESH = pl.DeviceIdType.MESH
HEAD = 128
NEG_FILL = -1e30
BIG = 1 << 30
VMEM_LIMIT = 54 * 1024 * 1024


class Sizes:
    def __init__(self, dp_count, seq_count, tok, width_q, width_k, groups):
        self.groups = groups
        self.S = seq_count
        self.Z = width_k // HEAD
        self.X = dp_count // self.Z
        self.tok = tok
        self.slots = 2 * tok // groups
        self.seg = 3 * dp_count * tok // (2 * groups)
        self.G = width_q // width_k
        self.qw = self.G * HEAD
        self.heads = (self.G - 2, 1, 1)
        self.first_head = (0, self.G - 2, self.G - 1)
        self.widths = (self.heads[0] * HEAD + 2 * HEAD, HEAD, HEAD)
        self.flat = self.groups * self.slots
        self.per_s = self.X * self.Z * self.slots
        self.rows = self.S * self.seg
        self.blk = 2 * self.seg // 3
        self.nb = self.rows // self.blk
        self.pad = 3 * self.blk
        self.wide = 4 * self.blk
        order = [0]
        for dist in range(1, self.Z // 2 + 1):
            order.append(dist)
            if self.Z - dist != dist:
                order.append(self.Z - dist)
        self.order = order
        if self.Z == 8:
            fine = ((0, 1), (1, 3), (3, 5), (5, 7), (7, 8))
            self.in_runs = (fine, ((0, 5), (5, 8)), ((0, 5), (5, 8)))
            self.out_runs = (((5, 8), (0, 5)), ((5, 8), (0, 5)), ((5, 8), (1, 5), (0, 1)))
        else:
            runs = ((0, 1), (1, self.Z))
            self.in_runs = (runs,) * 3
            self.out_runs = (runs[::-1],) * 3


def greet(n, x, z, s):
    barrier = pltpu.get_barrier_semaphore()
    plane = x * n.S + s
    count = n.X * n.S

    def one_plane(t, carry):
        p = lax.rem(plane + t, count)
        pl.semaphore_signal(
            barrier, inc=1, device_id=((p // n.S) * n.Z + z, lax.rem(p, n.S)), device_id_type=MESH
        )
        return carry

    lax.fori_loop(1, count, one_plane, 0)

    def one_line(t, carry):
        zt = lax.rem(z + t, n.Z)
        pl.semaphore_signal(barrier, inc=1, device_id=(x * n.Z + zt, s), device_id_type=MESH)
        return carry

    lax.fori_loop(1, n.Z, one_line, 0)
    pl.semaphore_wait(barrier, count - 1 + n.Z - 1)


def fused_kernel(n, offsets_ref, lengths_ref, q_ref, k_ref, v_ref, out_ref, *scratch):
    scratch = list(scratch)

    def take(count):
        found = scratch[:count]
        del scratch[:count]
        return found

    zb, sb, rc, qbuf, ub, rb, fb = (take(3) for _ in range(7))
    kbuf, vbuf, strip, top, acc, kpos, qspan, qlow, obuf, idx_rows, idx_cols, dst_rows, dst_cols = take(13)
    zsend, zrecv, psend, precv, usend, urecv, fsend, frecv = scratch
    dp, s = lax.axis_index("dp"), lax.axis_index("seq")
    x, z = dp // n.Z, lax.rem(dp, n.Z)
    plane = x * n.S + s
    count = n.X * n.S
    mine = s * n.X + x
    blk, wide = n.blk, n.wide
    half = min(128, blk)
    gain = HEAD ** -0.5 * math.log2(math.e)
    least = -(1 << 31)
    bf, f32, i32 = jnp.bfloat16, jnp.float32, jnp.int32

    def done(ref, sem):
        pltpu.make_async_copy(ref, ref, sem).wait()

    def remote(src, dst, send, recv, dp_to, s_to):
        pltpu.make_async_remote_copy(
            src_ref=src, dst_ref=dst, send_sem=send, recv_sem=recv,
            device_id=(dp_to, s_to), device_id_type=MESH,
        ).start()

    def to_plane(body):
        def one(t, carry):
            p = lax.rem(plane + t, count)
            body(p // n.S, lax.rem(p, n.S))
            return carry

        lax.fori_loop(1, count, one, 0)

    def z_of(place):
        return lax.rem(z - n.order[place] + n.Z, n.Z)

    def z_start(piece, place):
        zt = z if place == 0 else lax.rem(z + n.order[place], n.Z)
        hw = n.heads[piece] * HEAD
        first = pl.multiple_of(zt * n.qw + n.first_head[piece] * HEAD, HEAD)
        found = [(q_ref.at[:, pl.ds(first, hw)], zb[piece].at[place, :, pl.ds(0, hw)])]
        if piece == 0:
            cols = pl.ds(pl.multiple_of(zt * HEAD, HEAD), HEAD)
            found.append((k_ref.at[:, cols], zb[0].at[place, :, pl.ds(hw, HEAD)]))
            found.append((v_ref.at[:, cols], zb[0].at[place, :, pl.ds(hw + HEAD, HEAD)]))
        for src, dst in found:
            if place == 0:
                pltpu.make_async_copy(src, dst, zrecv.at[piece, 0]).start()
            else:
                remote(src, dst, zsend.at[piece, place], zrecv.at[piece, place], x * n.Z + zt, s)

    def iota(shape, dim):
        return lax.broadcasted_iota(i32, shape, dim)

    def exact(a, b, contract):
        high = jnp.floor(a * (1.0 / 16.0)) * 16.0
        dims = (contract, ((), ()))
        return lax.dot_general(high.astype(bf), b, dims, preferred_element_type=f32) + lax.dot_general(
            (a - high).astype(bf), b, dims, preferred_element_type=f32
        )

    def tables():
        groups, flat = n.groups, n.flat
        loads = [offsets_ref[pl.ds((x * n.Z + z_of(p)) * n.S + s, 1), :] for p in range(n.Z)]
        starts = jnp.concatenate(loads, axis=0).astype(f32)
        slot_lane, slot_sub = iota((1, flat), 1), iota((flat, 1), 0)
        owner = iota((flat, groups), 0) // n.slots
        of = iota((flat, groups), 1)
        same, after = (owner == of).astype(bf), (owner + 1 == of).astype(bf)
        nt = ((1,), (1,))
        for ref, slot, swap in ((idx_rows, slot_lane, False), (idx_cols, slot_sub, True)):
            pair = []
            for table in (same, after):
                if swap:
                    pair.append(lax.dot_general(table, starts.astype(bf), (nt, ((), ())), preferred_element_type=f32))
                else:
                    pair.append(lax.dot_general(starts.astype(bf), table, (nt, ((), ())), preferred_element_type=f32))
            begin = pair[0].astype(i32) + slot % n.slots
            end = pair[1].astype(i32) + jnp.where(slot // n.slots == groups - 1, n.tok, 0)
            ref[...] = jnp.where(begin < end, begin, -1)

        devices = n.X * n.Z * n.S
        column = iota((8, groups), 1)
        sign = jnp.where(column == plane + 1, 1.0, 0.0) - jnp.where(column == plane, 1.0, 0.0)
        counts = lax.dot_general(
            sign.astype(bf), offsets_ref[...].astype(f32).astype(bf), (nt, ((), ())), preferred_element_type=f32
        ) + jnp.where(plane == groups - 1, float(n.tok), 0.0)
        fa, fb_ = iota((devices, devices), 0), iota((devices, devices), 1)
        sa, sb_ = fa % n.S, fb_ % n.S
        few = counts.astype(bf)
        before = jnp.dot(few, ((sa == sb_) & (fa < fb_)).astype(bf), preferred_element_type=f32)
        totals = jnp.dot(few, (sa == sb_).astype(bf), preferred_element_type=f32)
        bases = jnp.dot(few, (sa < sb_).astype(bf), preferred_element_type=f32)

        pick_s = (iota((n.S, devices), 1) % n.S == iota((n.S, devices), 0)).astype(f32)
        cut = pick_s * before[0:1, :]
        cut_counts = pick_s * counts[0:1, :]
        flat_s = n.per_s
        at = iota((flat_s, devices), 0) // n.slots
        place = at % n.Z
        steps = (place + 1) // 2
        shift = jnp.where(place % 2 == 1, steps, n.Z - steps)
        z_at = (z - shift + 2 * n.Z) % n.Z
        line = (((at // n.Z) * n.Z + z_at) == iota((flat_s, devices), 1) // n.S).astype(bf)
        high = jnp.floor(cut * (1.0 / 16.0)) * 16.0
        three = [a.astype(bf) for a in (high, cut - high, cut_counts)]
        for ref, swap in ((dst_rows, False), (dst_cols, True)):
            got = []
            for a in three:
                pair = (line, a) if swap else (a, line)
                got.append(lax.dot_general(*pair, (nt, ((), ())), preferred_element_type=f32))
            slot = iota((flat_s, 1), 0) if swap else iota((1, flat_s), 1)
            slot = slot % n.slots
            ref[...] = jnp.where(slot < got[2].astype(i32), (got[0] + got[1]).astype(i32) + slot, -1)

        lens = jnp.broadcast_to(lengths_ref[pl.ds(plane, 1), :].astype(f32), (8, lengths_ref.shape[1]))
        docs = lengths_ref.shape[1]
        upto = (iota((docs, docs), 0) <= iota((docs, docs), 1)).astype(bf)
        ends = exact(lens, upto, ((1,), (0,)))[0:1, :].astype(i32)
        totals, bases = totals[0:1, :].astype(i32), bases[0:1, :].astype(i32)
        kpos[:, 0 : n.pad] = jnp.full((1, n.pad), BIG + least, i32)
        for k in range(n.S):
            tot, base = totals[:, k : k + 1], bases[:, k : k + 1]
            r = iota((1, n.seg), 1)
            at = n.pad + k * n.seg
            kpos[:, at : at + n.seg] = jnp.where(r < tot, base + r, BIG) + least
            r = iota((n.seg, docs), 0)
            pos = jnp.where(r < tot, base + r, -1)
            low = jnp.max(jnp.where(ends <= pos, ends, 0), axis=1, keepdims=True)
            low = jnp.broadcast_to(low, (n.seg, half))
            r = iota((n.seg, half), 0)
            pos = jnp.where(r < tot, base + r, -1)
            qlow[k * n.seg : (k + 1) * n.seg, :] = low
            qspan[k * n.seg : (k + 1) * n.seg, :] = pos - low + least

    lane = iota((n.flat, n.tok), 1)

    def in_run(piece, run, after=None):
        first, last = n.in_runs[piece][run]
        for place in range(first, last):
            done(zb[piece].at[place], zrecv.at[piece, place])
            if after is not None and place:
                z_start(after, place)
            pick = (lane == idx_cols[:, place : place + 1]).astype(bf)
            padded = jnp.dot(pick, zb[piece][place], preferred_element_type=f32).astype(bf)
            sb[piece][:, place] = padded.reshape(n.groups, n.slots, n.widths[piece])
        run_of = pl.ds(first, last - first)
        pltpu.make_async_copy(sb[piece].at[plane, run_of], rc[piece].at[mine, run_of], precv.at[piece]).start()
        to_plane(
            lambda xt, st: remote(
                sb[piece].at[xt * n.S + st, run_of], rc[piece].at[mine, run_of],
                psend.at[piece, run], precv.at[piece], xt * n.Z + z, st,
            )
        )

    def compact(piece):
        done(rc[piece], precv.at[piece])
        sub = iota((n.seg, n.per_s), 0)
        hw = n.heads[piece] * HEAD
        for k in range(n.S):
            pick = (sub == dst_rows[k : k + 1, :]).astype(bf)
            block = rc[piece][k * n.X : (k + 1) * n.X].reshape(n.per_s, n.widths[piece])
            comp = jnp.dot(pick, block, preferred_element_type=f32).astype(bf)
            for h in range(n.heads[piece]):
                qbuf[piece][h, k * n.seg : (k + 1) * n.seg, :] = comp[:, h * HEAD : (h + 1) * HEAD]
            if piece == 0:
                at = n.pad + k * n.seg
                kbuf[at : at + n.seg, :] = comp[:, hw : hw + HEAD]
                vbuf[at : at + n.seg, 0:HEAD] = comp[:, hw + HEAD :]

    def attend(piece, i, rows):
        heads = n.heads[piece]
        start = pl.multiple_of(i * rows, rows)
        here = pl.ds(0, heads * rows)
        top[here, :] = jnp.full((heads * rows, half), NEG_FILL, f32)
        acc[here, :] = jnp.zeros((heads * rows, 2 * HEAD), f32)
        chunks = ((i + 1) * rows + wide - 1) // wide

        def at_keys(j):
            return pl.multiple_of((i + 1) * rows - wide * (j + 1) + n.pad, blk)

        def scores(j, carry):
            queries = qbuf[piece][:, pl.ds(start, rows), :].reshape(heads * rows, HEAD)
            sc = lax.dot_general(
                queries, kbuf[pl.ds(at_keys(j), wide), :], (((1,), (1,)), ((), ())), preferred_element_type=f32
            )
            span, low = qspan[pl.ds(start, rows), :], qlow[pl.ds(start, rows), :]
            k_pos = kpos[:, pl.ds(at_keys(j), wide)]
            best = top[here, :]
            for col in range(0, wide, half):
                allowed = (k_pos[:, col : col + half] - low) <= span
                part = jnp.where(
                    allowed[None], sc[:, col : col + half].reshape(heads, rows, half), NEG_FILL
                ).reshape(heads * rows, half)
                strip[j, here, col : col + half] = part
                best = jnp.maximum(best, part)
            top[here, :] = best
            return carry

        lax.fori_loop(0, chunks, scores, 0)
        top[here, :] = jnp.broadcast_to(jnp.max(top[here, :], axis=1, keepdims=True) * gain, (heads * rows, half))

        def weigh(j, carry):
            row = top[here, :]
            pieces = [
                jnp.exp2(strip[j, here, col : col + half] * gain - row).astype(bf) for col in range(0, wide, half)
            ]
            acc[here, :] += jnp.dot(
                jnp.concatenate(pieces, axis=1), vbuf[pl.ds(at_keys(j), wide), :], preferred_element_type=f32
            )
            return carry

        lax.fori_loop(0, chunks, weigh, 0)
        denom = acc[here, HEAD:]
        result = (acc[here, :HEAD] / jnp.where(denom > 0.0, denom, 1.0)).astype(bf)
        for h in range(heads):
            obuf[pl.ds(start, rows), h * HEAD : (h + 1) * HEAD] = result[h * rows : (h + 1) * rows]

    def out_all(piece):
        hw = n.heads[piece] * HEAD
        wide_lane = iota((n.per_s, n.seg), 1)
        for k in range(n.S):
            pick = (wide_lane == dst_cols[:, k : k + 1]).astype(bf)
            spread = jnp.dot(
                pick, obuf[k * n.seg : (k + 1) * n.seg, 0:hw], preferred_element_type=f32
            ).astype(bf)
            ub[piece][k] = spread.reshape(n.X, n.Z, n.slots, hw)
        for run, (first, last) in enumerate(n.out_runs[piece]):
            run_of = pl.ds(first, last - first)
            pltpu.make_async_copy(
                ub[piece].at[s, x, run_of], rb[piece].at[plane, run_of], urecv.at[piece, run]
            ).start()
            to_plane(
                lambda xt, st: remote(
                    ub[piece].at[st, xt, run_of], rb[piece].at[plane, run_of],
                    usend.at[piece, run], urecv.at[piece, run], xt * n.Z + z, st,
                )
            )

    tall = iota((n.tok, n.flat), 0)

    def hand_back(piece, run):
        first, last = n.out_runs[piece][run]
        hw = n.heads[piece] * HEAD
        done(rb[piece].at[:, pl.ds(first, last - first)], urecv.at[piece, run])
        cols = pl.ds(pl.multiple_of(z * n.qw + n.first_head[piece] * HEAD, HEAD), hw)
        for place in reversed(range(first, last)):
            pick = (tall == idx_rows[place : place + 1, :]).astype(bf)
            fb[piece][place] = jnp.dot(
                pick, rb[piece][:, place].reshape(n.flat, hw), preferred_element_type=f32
            ).astype(bf)
            if place == 0:
                pltpu.make_async_copy(fb[piece].at[0], out_ref.at[:, cols], frecv.at[piece, 0]).start()
            else:
                remote(
                    fb[piece].at[place], out_ref.at[:, cols],
                    fsend.at[piece, place], frecv.at[piece, place], x * n.Z + z_of(place), s,
                )

    for piece in range(3):
        z_start(piece, 0)
    greet(n, x, z, s)
    for place in range(1, n.Z):
        z_start(0, place)
    tables()
    kbuf[0 : n.pad, :] = jnp.zeros((n.pad, HEAD), bf)
    vbuf[:, 0:HEAD] = jnp.zeros((n.rows + n.pad, HEAD), bf)
    vbuf[:, HEAD:] = jnp.ones((n.rows + n.pad, HEAD), bf)

    for run in range(len(n.in_runs[0])):
        in_run(0, run, 1)
    compact(0)

    def with_runs(t, plan):
        for when, work in plan:

            @pl.when(t == when)
            def _(work=work):
                work()

    first_plan = (
        (2, lambda: in_run(1, 0, 2)),
        (5, lambda: in_run(1, 1, 2)),
        (7, lambda: in_run(2, 0)),
        (9, lambda: in_run(2, 1)),
    )

    def first_block(t, carry):
        attend(0, t, blk)
        with_runs(t, first_plan)
        return carry

    lax.fori_loop(0, n.nb, first_block, 0)
    out_all(0)
    compact(1)
    half_nb = n.nb // 2

    def second_block(t, carry):
        attend(1, t, 2 * blk)
        return carry

    lax.fori_loop(0, half_nb, second_block, 0)
    out_all(1)
    compact(2)
    hand_back(0, 0)

    def third_block(t, carry):
        attend(2, t, 2 * blk)
        return carry

    lax.fori_loop(0, half_nb, third_block, 0)
    out_all(2)
    for piece in range(3):
        for run in range(len(n.out_runs[piece])):
            if (piece, run) != (0, 0):
                hand_back(piece, run)

    for piece in range(3):
        for place in range(n.Z):
            done(fb[piece].at[place], frecv.at[piece, place])
            if place:
                done(fb[piece].at[place], fsend.at[piece, place])
                done(zb[piece].at[place], zsend.at[piece, place])
        for run, (first, last) in enumerate(n.in_runs[piece]):
            done(sb[piece].at[pl.ds(0, count - 1), pl.ds(first, last - first)], psend.at[piece, run])
        for run, (first, last) in enumerate(n.out_runs[piece]):
            done(rb[piece].at[pl.ds(0, count - 1), pl.ds(first, last - first)], usend.at[piece, run])


def fused(n, offsets, lengths, q, k, v):
    vmem = pl.BlockSpec(memory_space=pltpu.VMEM)
    anyspace = pl.BlockSpec(memory_space=pl.ANY)
    half = min(128, n.blk)
    chunks = (n.nb + 3) // 4
    bf, f32 = jnp.bfloat16, jnp.float32
    sem = pltpu.SemaphoreType.DMA
    senders = n.X * n.S
    outs = [h * HEAD for h in n.heads]

    def each(widths, *dims):
        return [pltpu.VMEM(dims + (w,), bf) for w in widths]

    most = max(n.heads[0] * n.blk, 2 * n.blk)
    return pl.pallas_call(
        functools.partial(fused_kernel, n),
        out_shape=jax.ShapeDtypeStruct((n.tok, n.Z * n.qw), bf),
        in_specs=[vmem, vmem, anyspace, anyspace, anyspace],
        out_specs=vmem,
        scratch_shapes=each(n.widths, n.Z, n.tok)
        + each(n.widths, n.groups, n.Z, n.slots)
        + each(n.widths, senders, n.Z, n.slots)
        + [pltpu.VMEM((h, n.rows, HEAD), bf) for h in n.heads]
        + each(outs, n.S, n.X, n.Z, n.slots)
        + each(outs, n.groups, n.Z, n.slots)
        + each(outs, n.Z, n.tok)
        + [
            pltpu.VMEM((n.rows + n.pad, HEAD), bf),
            pltpu.VMEM((n.rows + n.pad, 2 * HEAD), bf),
            pltpu.VMEM((chunks, most, n.wide), f32),
            pltpu.VMEM((most, half), f32),
            pltpu.VMEM((most, 2 * HEAD), f32),
            pltpu.VMEM((1, n.rows + n.pad), jnp.int32),
            pltpu.VMEM((n.rows, half), jnp.int32),
            pltpu.VMEM((n.rows, half), jnp.int32),
            pltpu.VMEM((n.rows, outs[0]), bf),
            pltpu.VMEM((n.Z, n.flat), jnp.int32),
            pltpu.VMEM((n.flat, n.Z), jnp.int32),
            pltpu.VMEM((n.S, n.per_s), jnp.int32),
            pltpu.VMEM((n.per_s, n.S), jnp.int32),
            sem((3, n.Z)),
            sem((3, n.Z)),
            sem((3, 5)),
            sem((3,)),
            sem((3, 5)),
            sem((3, 5)),
            sem((3, n.Z)),
            sem((3, n.Z)),
        ],
        compiler_params=pltpu.CompilerParams(
            collective_id=0, has_side_effects=True, vmem_limit_bytes=VMEM_LIMIT
        ),
        name="route_and_attend",
    )(offsets, lengths, q, k, v)


def on_device(queries, keys, values, row_offsets, doc_lengths):
    n = Sizes(
        lax.axis_size("dp"), lax.axis_size("seq"), queries.shape[0], queries.shape[1], keys.shape[1],
        row_offsets.shape[1],
    )
    return fused(n, row_offsets, doc_lengths, queries, keys, values)


def solution(mesh):
    return jax.shard_map(
        on_device,
        mesh=mesh,
        in_specs=(P(("dp", "seq"), None), P(("dp", "seq"), None), P(("dp", "seq"), None), P(), P()),
        out_specs=P(("dp", "seq"), None),
        check_vma=False,
    )
```

```python
import functools
import math

import jax
import jax.numpy as jnp
from jax import lax
from jax.experimental import pallas as pl
from jax.experimental.pallas import tpu as pltpu
from jax.sharding import PartitionSpec as P

MESH = pl.DeviceIdType.MESH
HEAD = 128
NEG_FILL = -1e30
BIG = 1 << 30
VMEM_LIMIT = 58 * 1024 * 1024


class Sizes:
    def __init__(self, dp_count, seq_count, tok, width_q, width_k, groups):
        self.groups = groups
        self.S = seq_count
        self.Z = width_k // HEAD
        self.X = dp_count // self.Z
        self.tok = tok
        self.slots = 2 * tok // groups
        self.seg = 3 * dp_count * tok // (2 * groups)
        self.G = width_q // width_k
        self.qw = self.G * HEAD
        self.heads = (self.G - 2, 1, 1)
        self.first_head = (0, self.G - 2, self.G - 1)
        self.widths = (self.heads[0] * HEAD + 2 * HEAD, HEAD, HEAD)
        self.flat = self.groups * self.slots
        self.per_s = self.X * self.Z * self.slots
        self.rows = self.S * self.seg
        self.blk = 2 * self.seg // 3
        self.nb = self.rows // self.blk
        self.pad = 3 * self.blk
        self.wide = 4 * self.blk
        order = [0]
        for dist in range(1, self.Z // 2 + 1):
            order.append(dist)
            if self.Z - dist != dist:
                order.append(self.Z - dist)
        self.order = order
        if self.Z == 8:
            fine = ((0, 1), (1, 3), (3, 5), (5, 7), (7, 8))
            self.in_runs = (fine, ((0, 5), (5, 8)), ((0, 5), (5, 8)))
            self.out_runs = (((5, 8), (0, 5)), ((5, 8), (0, 5)), ((5, 8), (1, 5), (0, 1)))
        else:
            runs = ((0, 1), (1, self.Z))
            self.in_runs = (runs,) * 3
            self.out_runs = (runs[::-1],) * 3
        self.relay = self.X == 4 and self.S == 8
        self.zrelay = self.Z == 8

    def relayed(self, phase, piece, run):
        if phase == 0:
            return self.relay and (piece, run) != (0, len(self.in_runs[0]) - 1)
        return self.relay and piece < 2


def greet(n, x, z, s):
    barrier = pltpu.get_barrier_semaphore()
    plane = x * n.S + s
    count = n.X * n.S

    def one_plane(t, carry):
        p = lax.rem(plane + t, count)
        pl.semaphore_signal(
            barrier, inc=1, device_id=((p // n.S) * n.Z + z, lax.rem(p, n.S)), device_id_type=MESH
        )
        return carry

    lax.fori_loop(1, count, one_plane, 0)

    def one_line(t, carry):
        zt = lax.rem(z + t, n.Z)
        pl.semaphore_signal(barrier, inc=1, device_id=(x * n.Z + zt, s), device_id_type=MESH)
        return carry

    lax.fori_loop(1, n.Z, one_line, 0)
    pl.semaphore_wait(barrier, count - 1 + n.Z - 1)


def fused_kernel(n, offsets_ref, lengths_ref, q_ref, k_ref, v_ref, out_ref, *scratch):
    scratch = list(scratch)

    def take(count):
        found = scratch[:count]
        del scratch[:count]
        return found

    zb, sb, rc, qbuf, ub, rb, fb = (take(3) for _ in range(7))
    xrel = (take(3), take(3))
    yrel = (take(3), take(3))
    kbuf, vbuf, strip, top, acc, kpos, qspan, qlow, obuf, idx_rows, idx_cols, dst_rows, dst_cols = take(13)
    zsend, zrecv, psend, precv, usend, urecv, fsend, frecv, zrel, zs, zr, xs, xr, xf, ys, yr, yf = scratch
    dp, s = lax.axis_index("dp"), lax.axis_index("seq")
    x, z = dp // n.Z, lax.rem(dp, n.Z)
    plane = x * n.S + s
    count = n.X * n.S
    mine = s * n.X + x
    blk, wide = n.blk, n.wide
    half = min(128, blk)
    gain = HEAD ** -0.5 * math.log2(math.e)
    least = -(1 << 31)
    bf, f32, i32 = jnp.bfloat16, jnp.float32, jnp.int32

    def done(ref, sem):
        pltpu.make_async_copy(ref, ref, sem).wait()

    def remote(src, dst, send, recv, dp_to, s_to):
        pltpu.make_async_remote_copy(
            src_ref=src, dst_ref=dst, send_sem=send, recv_sem=recv,
            device_id=(dp_to, s_to), device_id_type=MESH,
        ).start()

    y, c = s // 2, lax.rem(s, 2)

    def to_plane(body, near):
        def one(t, carry):
            p = lax.rem(plane + t, count)
            body(p // n.S, lax.rem(p, n.S))
            return carry

        def one_near(t, carry):
            dx, dy = t // 6, lax.rem(t, 6) // 2
            dx, dy = dx + dx // 2, dy + dy // 2
            body(lax.rem(x + dx, 4), lax.rem(y + dy, 4) * 2 + lax.rem(c + t, 2))
            return carry

        if near:
            lax.fori_loop(1, 18, one_near, 0)
        else:
            lax.fori_loop(1, count, one, 0)

    def side(phase, piece, run):
        return (1, 3) if (phase + piece + run) % 2 == 0 else (3, 1)

    def runs_of(phase, piece, run):
        first, last = (n.in_runs, n.out_runs)[phase][piece][run]
        return pl.ds(first, last - first)

    def to_relays(phase, piece, run):
        ex, ey = side(phase, piece, run)
        part = runs_of(phase, piece, run)
        x_far, y_far = lax.rem(x + 2, 4), lax.rem(y + 2, 4)
        if phase == 0:
            src = sb[piece].at[pl.ds(x_far * n.S, n.S), part]
        else:
            src = ub[piece].at[:, x_far, part]
        remote(
            src, xrel[phase][piece].at[:, part], xs.at[phase, piece, run], xr.at[phase, piece, run],
            lax.rem(x + ex, 4) * n.Z + z, s,
        )
        for k, dx in enumerate((0, 1, 3)):
            xt = lax.rem(x + dx, 4)
            if phase == 0:
                src = sb[piece].at[pl.ds(xt * n.S + y_far * 2, 2), part]
            else:
                src = ub[piece].at[pl.ds(y_far * 2, 2), xt, part]
            remote(
                src, yrel[phase][piece].at[k, :, part], ys.at[phase, piece, run], yr.at[phase, piece, run],
                dp, lax.rem(y + ey, 4) * 2 + c,
            )

    def forward(phase, piece, run):
        if not n.relayed(phase, piece, run):
            return
        ex, ey = side(phase, piece, run)
        part = runs_of(phase, piece, run)
        x_from, x_to = lax.rem(x + 4 - ex, 4), lax.rem(x + ex, 4)
        y_from, y_to = lax.rem(y + 4 - ey, 4), lax.rem(y + ey, 4)

        def landing(xo, so):
            if phase == 0:
                return rc[piece].at[so * n.X + xo, part], precv.at[piece]
            return rb[piece].at[xo * n.S + so, part], urecv.at[piece, run]

        done(xrel[phase][piece].at[:, part], xr.at[phase, piece, run])

        def on_x(t, carry):
            st = lax.rem(s + t, n.S)
            dst, sem = landing(x_from, s)
            remote(xrel[phase][piece].at[st, part], dst, xf.at[phase, piece, run], sem, x_to * n.Z + z, st)
            return carry

        lax.fori_loop(0, n.S, on_x, 0)
        done(yrel[phase][piece].at[:, :, part], yr.at[phase, piece, run])

        def on_y(t, carry):
            k, side_c = t // 2, lax.rem(t, 2)
            dst, sem = landing(x, y_from * 2 + c)
            remote(
                yrel[phase][piece].at[k, side_c, part], dst, yf.at[phase, piece, run], sem,
                lax.rem(x + k + k // 2, 4) * n.Z + z, y_to * 2 + side_c,
            )
            return carry

        lax.fori_loop(0, 6, on_y, 0)

    def z_of(place):
        return lax.rem(z - n.order[place] + n.Z, n.Z)

    def z_start(piece, place):
        zt = z if place == 0 else lax.rem(z + n.order[place], n.Z)
        hw = n.heads[piece] * HEAD
        first = pl.multiple_of(zt * n.qw + n.first_head[piece] * HEAD, HEAD)

        def found(rows, to):
            got = [(q_ref.at[rows, pl.ds(first, hw)], to.at[:, pl.ds(0, hw)])]
            if piece == 0:
                cols = pl.ds(pl.multiple_of(zt * HEAD, HEAD), HEAD)
                got.append((k_ref.at[rows, cols], to.at[:, pl.ds(hw, HEAD)]))
                got.append((v_ref.at[rows, cols], to.at[:, pl.ds(hw + HEAD, HEAD)]))
            return got

        if n.zrelay and (piece, place) == (0, n.Z - 1):
            for k, via in enumerate((2, n.Z - 2)):
                for src, dst in found(pl.ds(k * n.tok // 2, n.tok // 2), zrel.at[k]):
                    remote(src, dst, zsend.at[0, place], zr.at[k], x * n.Z + lax.rem(z + via, n.Z), s)
            return
        for src, dst in found(pl.ds(0, n.tok), zb[piece].at[place]):
            if place == 0:
                pltpu.make_async_copy(src, dst, zrecv.at[piece, 0]).start()
            else:
                remote(src, dst, zsend.at[piece, place], zrecv.at[piece, place], x * n.Z + zt, s)

    def forward_z():
        for k, via in enumerate((2, n.Z - 2)):
            done(zrel.at[k], zr.at[k])
            remote(
                zrel.at[k], zb[0].at[n.Z - 1, pl.ds(k * n.tok // 2, n.tok // 2)],
                zs.at[k], zrecv.at[0, n.Z - 1], x * n.Z + lax.rem(z + via, n.Z), s,
            )

    def iota(shape, dim):
        return lax.broadcasted_iota(i32, shape, dim)

    def exact(a, b, contract):
        high = jnp.floor(a * (1.0 / 16.0)) * 16.0
        dims = (contract, ((), ()))
        return lax.dot_general(high.astype(bf), b, dims, preferred_element_type=f32) + lax.dot_general(
            (a - high).astype(bf), b, dims, preferred_element_type=f32
        )

    def tables():
        groups, flat = n.groups, n.flat
        loads = [offsets_ref[pl.ds((x * n.Z + z_of(p)) * n.S + s, 1), :] for p in range(n.Z)]
        starts = jnp.concatenate(loads, axis=0).astype(f32)
        slot_lane, slot_sub = iota((1, flat), 1), iota((flat, 1), 0)
        owner = iota((flat, groups), 0) // n.slots
        of = iota((flat, groups), 1)
        same, after = (owner == of).astype(bf), (owner + 1 == of).astype(bf)
        nt = ((1,), (1,))
        for ref, slot, swap in ((idx_rows, slot_lane, False), (idx_cols, slot_sub, True)):
            pair = []
            for table in (same, after):
                if swap:
                    pair.append(lax.dot_general(table, starts.astype(bf), (nt, ((), ())), preferred_element_type=f32))
                else:
                    pair.append(lax.dot_general(starts.astype(bf), table, (nt, ((), ())), preferred_element_type=f32))
            begin = pair[0].astype(i32) + slot % n.slots
            end = pair[1].astype(i32) + jnp.where(slot // n.slots == groups - 1, n.tok, 0)
            ref[...] = jnp.where(begin < end, begin, -1)

        devices = n.X * n.Z * n.S
        column = iota((8, groups), 1)
        sign = jnp.where(column == plane + 1, 1.0, 0.0) - jnp.where(column == plane, 1.0, 0.0)
        counts = lax.dot_general(
            sign.astype(bf), offsets_ref[...].astype(f32).astype(bf), (nt, ((), ())), preferred_element_type=f32
        ) + jnp.where(plane == groups - 1, float(n.tok), 0.0)
        fa, fb_ = iota((devices, devices), 0), iota((devices, devices), 1)
        sa, sb_ = fa % n.S, fb_ % n.S
        few = counts.astype(bf)
        before = jnp.dot(few, ((sa == sb_) & (fa < fb_)).astype(bf), preferred_element_type=f32)
        totals = jnp.dot(few, (sa == sb_).astype(bf), preferred_element_type=f32)
        bases = jnp.dot(few, (sa < sb_).astype(bf), preferred_element_type=f32)

        pick_s = (iota((n.S, devices), 1) % n.S == iota((n.S, devices), 0)).astype(f32)
        cut = pick_s * before[0:1, :]
        cut_counts = pick_s * counts[0:1, :]
        flat_s = n.per_s
        at = iota((flat_s, devices), 0) // n.slots
        place = at % n.Z
        steps = (place + 1) // 2
        shift = jnp.where(place % 2 == 1, steps, n.Z - steps)
        z_at = (z - shift + 2 * n.Z) % n.Z
        line = (((at // n.Z) * n.Z + z_at) == iota((flat_s, devices), 1) // n.S).astype(bf)
        high = jnp.floor(cut * (1.0 / 16.0)) * 16.0
        three = [a.astype(bf) for a in (high, cut - high, cut_counts)]
        for ref, swap in ((dst_rows, False), (dst_cols, True)):
            got = []
            for a in three:
                pair = (line, a) if swap else (a, line)
                got.append(lax.dot_general(*pair, (nt, ((), ())), preferred_element_type=f32))
            slot = iota((flat_s, 1), 0) if swap else iota((1, flat_s), 1)
            slot = slot % n.slots
            ref[...] = jnp.where(slot < got[2].astype(i32), (got[0] + got[1]).astype(i32) + slot, -1)

        lens = jnp.broadcast_to(lengths_ref[pl.ds(plane, 1), :].astype(f32), (8, lengths_ref.shape[1]))
        docs = lengths_ref.shape[1]
        upto = (iota((docs, docs), 0) <= iota((docs, docs), 1)).astype(bf)
        ends = exact(lens, upto, ((1,), (0,)))[0:1, :].astype(i32)
        totals, bases = totals[0:1, :].astype(i32), bases[0:1, :].astype(i32)
        kpos[:, 0 : n.pad] = jnp.full((1, n.pad), BIG + least, i32)
        for k in range(n.S):
            tot, base = totals[:, k : k + 1], bases[:, k : k + 1]
            r = iota((1, n.seg), 1)
            at = n.pad + k * n.seg
            kpos[:, at : at + n.seg] = jnp.where(r < tot, base + r, BIG) + least
            r = iota((n.seg, docs), 0)
            pos = jnp.where(r < tot, base + r, -1)
            low = jnp.max(jnp.where(ends <= pos, ends, 0), axis=1, keepdims=True)
            low = jnp.broadcast_to(low, (n.seg, half))
            r = iota((n.seg, half), 0)
            pos = jnp.where(r < tot, base + r, -1)
            qlow[k * n.seg : (k + 1) * n.seg, :] = low
            qspan[k * n.seg : (k + 1) * n.seg, :] = pos - low + least

    lane = iota((n.flat, n.tok), 1)

    def in_run(piece, run, after=None):
        first, last = n.in_runs[piece][run]
        for place in range(first, last):
            done(zb[piece].at[place], zrecv.at[piece, place])
            if after is not None and place:
                z_start(after, place)
            pick = (lane == idx_cols[:, place : place + 1]).astype(bf)
            padded = jnp.dot(pick, zb[piece][place], preferred_element_type=f32).astype(bf)
            sb[piece][:, place] = padded.reshape(n.groups, n.slots, n.widths[piece])
        run_of = pl.ds(first, last - first)
        if n.relayed(0, piece, run):
            to_relays(0, piece, run)
        pltpu.make_async_copy(sb[piece].at[plane, run_of], rc[piece].at[mine, run_of], precv.at[piece]).start()
        to_plane(
            lambda xt, st: remote(
                sb[piece].at[xt * n.S + st, run_of], rc[piece].at[mine, run_of],
                psend.at[piece, run], precv.at[piece], xt * n.Z + z, st,
            ),
            n.relayed(0, piece, run),
        )

    def compact(piece):
        done(rc[piece], precv.at[piece])
        sub = iota((n.seg, n.per_s), 0)
        hw = n.heads[piece] * HEAD
        for k in range(n.S):
            pick = (sub == dst_rows[k : k + 1, :]).astype(bf)
            block = rc[piece][k * n.X : (k + 1) * n.X].reshape(n.per_s, n.widths[piece])
            comp = jnp.dot(pick, block, preferred_element_type=f32).astype(bf)
            for h in range(n.heads[piece]):
                qbuf[piece][h, k * n.seg : (k + 1) * n.seg, :] = comp[:, h * HEAD : (h + 1) * HEAD]
            if piece == 0:
                at = n.pad + k * n.seg
                kbuf[at : at + n.seg, :] = comp[:, hw : hw + HEAD]
                vbuf[at : at + n.seg, 0:HEAD] = comp[:, hw + HEAD :]

    def attend(piece, i, rows):
        heads = n.heads[piece]
        start = pl.multiple_of(i * rows, rows)
        here = pl.ds(0, heads * rows)
        top[here, :] = jnp.full((heads * rows, half), NEG_FILL, f32)
        acc[here, :] = jnp.zeros((heads * rows, 2 * HEAD), f32)
        chunks = ((i + 1) * rows + wide - 1) // wide

        def at_keys(j):
            return pl.multiple_of((i + 1) * rows - wide * (j + 1) + n.pad, blk)

        def scores(j, carry):
            queries = qbuf[piece][:, pl.ds(start, rows), :].reshape(heads * rows, HEAD)
            sc = lax.dot_general(
                queries, kbuf[pl.ds(at_keys(j), wide), :], (((1,), (1,)), ((), ())), preferred_element_type=f32
            )
            span, low = qspan[pl.ds(start, rows), :], qlow[pl.ds(start, rows), :]
            k_pos = kpos[:, pl.ds(at_keys(j), wide)]
            best = top[here, :]
            for col in range(0, wide, half):
                allowed = (k_pos[:, col : col + half] - low) <= span
                part = jnp.where(
                    allowed[None], sc[:, col : col + half].reshape(heads, rows, half), NEG_FILL
                ).reshape(heads * rows, half)
                strip[j, here, col : col + half] = part
                best = jnp.maximum(best, part)
            top[here, :] = best
            return carry

        lax.fori_loop(0, chunks, scores, 0)
        top[here, :] = jnp.broadcast_to(jnp.max(top[here, :], axis=1, keepdims=True) * gain, (heads * rows, half))

        def weigh(j, carry):
            row = top[here, :]
            pieces = [
                jnp.exp2(strip[j, here, col : col + half] * gain - row).astype(bf) for col in range(0, wide, half)
            ]
            acc[here, :] += jnp.dot(
                jnp.concatenate(pieces, axis=1), vbuf[pl.ds(at_keys(j), wide), :], preferred_element_type=f32
            )
            return carry

        lax.fori_loop(0, chunks, weigh, 0)
        denom = acc[here, HEAD:]
        result = (acc[here, :HEAD] / jnp.where(denom > 0.0, denom, 1.0)).astype(bf)
        for h in range(heads):
            obuf[pl.ds(start, rows), h * HEAD : (h + 1) * HEAD] = result[h * rows : (h + 1) * rows]

    def out_all(piece):
        hw = n.heads[piece] * HEAD
        wide_lane = iota((n.per_s, n.seg), 1)
        for k in range(n.S):
            pick = (wide_lane == dst_cols[:, k : k + 1]).astype(bf)
            spread = jnp.dot(
                pick, obuf[k * n.seg : (k + 1) * n.seg, 0:hw], preferred_element_type=f32
            ).astype(bf)
            ub[piece][k] = spread.reshape(n.X, n.Z, n.slots, hw)
        for run, (first, last) in enumerate(n.out_runs[piece]):
            run_of = pl.ds(first, last - first)
            if n.relayed(1, piece, run):
                to_relays(1, piece, run)
            pltpu.make_async_copy(
                ub[piece].at[s, x, run_of], rb[piece].at[plane, run_of], urecv.at[piece, run]
            ).start()
            to_plane(
                lambda xt, st: remote(
                    ub[piece].at[st, xt, run_of], rb[piece].at[plane, run_of],
                    usend.at[piece, run], urecv.at[piece, run], xt * n.Z + z, st,
                ),
                n.relayed(1, piece, run),
            )

    tall = iota((n.tok, n.flat), 0)

    def hand_back(piece, run):
        first, last = n.out_runs[piece][run]
        hw = n.heads[piece] * HEAD
        done(rb[piece].at[:, pl.ds(first, last - first)], urecv.at[piece, run])
        cols = pl.ds(pl.multiple_of(z * n.qw + n.first_head[piece] * HEAD, HEAD), hw)
        for place in reversed(range(first, last)):
            pick = (tall == idx_rows[place : place + 1, :]).astype(bf)
            fb[piece][place] = jnp.dot(
                pick, rb[piece][:, place].reshape(n.flat, hw), preferred_element_type=f32
            ).astype(bf)
            if place == 0:
                pltpu.make_async_copy(fb[piece].at[0], out_ref.at[:, cols], frecv.at[piece, 0]).start()
            else:
                remote(
                    fb[piece].at[place], out_ref.at[:, cols],
                    fsend.at[piece, place], frecv.at[piece, place], x * n.Z + z_of(place), s,
                )

    for piece in range(3):
        z_start(piece, 0)
    greet(n, x, z, s)
    for place in (1, 2, 7, 3, 4, 5, 6) if n.zrelay else range(1, n.Z):
        z_start(0, place)
    tables()
    kbuf[0 : n.pad, :] = jnp.zeros((n.pad, HEAD), bf)
    vbuf[:, 0:HEAD] = jnp.zeros((n.rows + n.pad, HEAD), bf)
    vbuf[:, HEAD:] = jnp.ones((n.rows + n.pad, HEAD), bf)

    for run in range(len(n.in_runs[0])):
        in_run(0, run, 1)
        if n.zrelay and run == 1:
            forward_z()
        if run:
            forward(0, 0, run - 1)
    compact(0)

    def with_runs(t, plan):
        for when, work in plan:

            @pl.when(t == when)
            def _(work=work):
                work()

    first_plan = (
        (2, lambda: in_run(1, 0, 2)),
        (3, lambda: forward(0, 1, 0)),
        (5, lambda: in_run(1, 1, 2)),
        (6, lambda: forward(0, 1, 1)),
        (7, lambda: in_run(2, 0)),
        (8, lambda: forward(0, 2, 0)),
        (9, lambda: in_run(2, 1)),
        (10, lambda: forward(0, 2, 1)),
    )

    def first_block(t, carry):
        attend(0, t, blk)
        with_runs(t, first_plan)
        return carry

    lax.fori_loop(0, n.nb, first_block, 0)
    out_all(0)
    compact(1)
    half_nb = n.nb // 2

    def second_block(t, carry):
        attend(1, t, 2 * blk)
        with_runs(t, ((2, lambda: forward(1, 0, 0)), (4, lambda: forward(1, 0, 1))))
        return carry

    lax.fori_loop(0, half_nb, second_block, 0)
    out_all(1)
    compact(2)
    hand_back(0, 0)

    def third_block(t, carry):
        attend(2, t, 2 * blk)
        with_runs(
            t,
            (
                (2, lambda: forward(1, 1, 0)),
                (3, lambda: hand_back(0, 1)),
                (4, lambda: forward(1, 1, 1)),
            ),
        )
        return carry

    lax.fori_loop(0, half_nb, third_block, 0)
    out_all(2)
    for piece in range(3):
        for run in range(len(n.out_runs[piece])):
            if piece:
                hand_back(piece, run)

    for piece in range(3):
        for place in range(n.Z):
            done(fb[piece].at[place], frecv.at[piece, place])
            if place:
                done(fb[piece].at[place], fsend.at[piece, place])
                done(zb[piece].at[place], zsend.at[piece, place])
        for phase, runs in ((0, n.in_runs[piece]), (1, n.out_runs[piece])):
            for run, (first, last) in enumerate(runs):
                part = pl.ds(first, last - first)
                relayed = n.relayed(phase, piece, run)
                sent = pl.ds(0, 17 if relayed else count - 1)
                if phase == 0:
                    done(sb[piece].at[sent, part], psend.at[piece, run])
                else:
                    done(rb[piece].at[sent, part], usend.at[piece, run])
                if relayed:
                    for sem in (xs, xf):
                        done(xrel[phase][piece].at[:, part], sem.at[phase, piece, run])
                    for sem in (ys, yf):
                        done(yrel[phase][piece].at[:, :, part], sem.at[phase, piece, run])
    if n.zrelay:
        for k in range(2):
            done(zrel.at[k], zs.at[k])


def fused(n, offsets, lengths, q, k, v):
    vmem = pl.BlockSpec(memory_space=pltpu.VMEM)
    anyspace = pl.BlockSpec(memory_space=pl.ANY)
    half = min(128, n.blk)
    chunks = (n.nb + 3) // 4
    bf, f32 = jnp.bfloat16, jnp.float32
    sem = pltpu.SemaphoreType.DMA
    senders = n.X * n.S
    outs = [h * HEAD for h in n.heads]

    def each(widths, *dims):
        return [pltpu.VMEM(dims + (w,), bf) for w in widths]

    most = max(n.heads[0] * n.blk, 2 * n.blk)
    return pl.pallas_call(
        functools.partial(fused_kernel, n),
        out_shape=jax.ShapeDtypeStruct((n.tok, n.Z * n.qw), bf),
        in_specs=[vmem, vmem, anyspace, anyspace, anyspace],
        out_specs=vmem,
        scratch_shapes=each(n.widths, n.Z, n.tok)
        + each(n.widths, n.groups, n.Z, n.slots)
        + each(n.widths, senders, n.Z, n.slots)
        + [pltpu.VMEM((h, n.rows, HEAD), bf) for h in n.heads]
        + each(outs, n.S, n.X, n.Z, n.slots)
        + each(outs, n.groups, n.Z, n.slots)
        + each(outs, n.Z, n.tok)
        + each(n.widths, n.S, n.Z, n.slots)
        + each(outs[:2], n.S, n.Z, n.slots)
        + each(outs[2:], 1, 1, n.slots)
        + each(n.widths, 3, 2, n.Z, n.slots)
        + each(outs[:2], 3, 2, n.Z, n.slots)
        + each(outs[2:], 1, 1, 1, n.slots)
        + [
            pltpu.VMEM((n.rows + n.pad, HEAD), bf),
            pltpu.VMEM((n.rows + n.pad, 2 * HEAD), bf),
            pltpu.VMEM((chunks, most, n.wide), f32),
            pltpu.VMEM((most, half), f32),
            pltpu.VMEM((most, 2 * HEAD), f32),
            pltpu.VMEM((1, n.rows + n.pad), jnp.int32),
            pltpu.VMEM((n.rows, half), jnp.int32),
            pltpu.VMEM((n.rows, half), jnp.int32),
            pltpu.VMEM((n.rows, outs[0]), bf),
            pltpu.VMEM((n.Z, n.flat), jnp.int32),
            pltpu.VMEM((n.flat, n.Z), jnp.int32),
            pltpu.VMEM((n.S, n.per_s), jnp.int32),
            pltpu.VMEM((n.per_s, n.S), jnp.int32),
            sem((3, n.Z)),
            sem((3, n.Z)),
            sem((3, 5)),
            sem((3,)),
            sem((3, 5)),
            sem((3, 5)),
            sem((3, n.Z)),
            sem((3, n.Z)),
            pltpu.VMEM((2, n.tok // 2, n.widths[0]), bf),
            sem((2,)),
            sem((2,)),
        ]
        + [sem((2, 3, 5))] * 6,
        compiler_params=pltpu.CompilerParams(
            collective_id=0, has_side_effects=True, vmem_limit_bytes=VMEM_LIMIT
        ),
        name="route_and_attend",
    )(offsets, lengths, q, k, v)


def on_device(queries, keys, values, row_offsets, doc_lengths):
    n = Sizes(
        lax.axis_size("dp"), lax.axis_size("seq"), queries.shape[0], queries.shape[1], keys.shape[1],
        row_offsets.shape[1],
    )
    return fused(n, row_offsets, doc_lengths, queries, keys, values)


def solution(mesh):
    return jax.shard_map(
        on_device,
        mesh=mesh,
        in_specs=(P(("dp", "seq"), None), P(("dp", "seq"), None), P(("dp", "seq"), None), P(), P()),
        out_specs=P(("dp", "seq"), None),
        check_vma=False,
    )
```

```python
import functools
import math

import jax
import jax.numpy as jnp
from jax import lax
from jax.experimental import pallas as pl
from jax.experimental.pallas import tpu as pltpu
from jax.sharding import PartitionSpec as P

MESH = pl.DeviceIdType.MESH
HEAD = 128
NEG_FILL = -1e30
APART = -float(1 << 40)
VMEM_LIMIT = 54 * 1024 * 1024


class Sizes:
    def __init__(self, dp_count, seq_count, tok, width_q, width_k, groups):
        self.groups = groups
        self.S = seq_count
        self.Z = width_k // HEAD
        self.X = dp_count // self.Z
        self.tok = tok
        self.slots = 2 * tok // groups
        self.seg = 3 * dp_count * tok // (2 * groups)
        self.G = width_q // width_k
        self.qw = self.G * HEAD
        self.heads = (self.G // 2, self.G // 2)
        self.first_head = (0, self.G // 2)
        self.widths = (self.heads[0] * HEAD + 2 * HEAD, self.heads[1] * HEAD)
        self.flat = self.groups * self.slots
        self.per_s = self.X * self.Z * self.slots
        self.rows = self.S * self.seg
        self.blk = 2 * self.seg // 3
        self.nb = self.rows // self.blk
        self.pad = 3 * self.blk
        self.wide = 4 * self.blk
        order = [0]
        for dist in range(1, self.Z // 2 + 1):
            order.append(dist)
            if self.Z - dist != dist:
                order.append(self.Z - dist)
        self.order = order
        if self.Z == 8:
            fine = ((0, 1), (1, 3), (3, 5), (5, 7), (7, 8))
            self.in_runs = (fine, ((0, 3), (3, 5), (5, 8)))
            self.out_runs = (((5, 8), (3, 5), (0, 3)), ((7, 8), (5, 7), (3, 5), (0, 3)))
        else:
            runs = ((0, 1), (1, self.Z))
            self.in_runs = (runs,) * 2
            self.out_runs = (runs[::-1],) * 2


def greet(n, x, z, s):
    barrier = pltpu.get_barrier_semaphore()
    plane = x * n.S + s
    count = n.X * n.S

    def one_plane(t, carry):
        p = lax.rem(plane + t, count)
        pl.semaphore_signal(
            barrier, inc=1, device_id=((p // n.S) * n.Z + z, lax.rem(p, n.S)), device_id_type=MESH
        )
        return carry

    lax.fori_loop(1, count, one_plane, 0)

    def one_line(t, carry):
        zt = lax.rem(z + t, n.Z)
        pl.semaphore_signal(barrier, inc=1, device_id=(x * n.Z + zt, s), device_id_type=MESH)
        return carry

    lax.fori_loop(1, n.Z, one_line, 0)
    pl.semaphore_wait(barrier, count - 1 + n.Z - 1)


def fused_kernel(n, offsets_ref, lengths_ref, q_ref, k_ref, v_ref, out_ref, *scratch):
    scratch = list(scratch)

    def take(count):
        found = scratch[:count]
        del scratch[:count]
        return found

    zb, sb, rc, qbuf, ub, rb, fb = (take(2) for _ in range(7))
    kbuf, vbuf, qdoc, strip, top, acc, obuf, idx_rows, idx_cols, dst_rows, dst_cols = take(11)
    zsend, zrecv, psend, precv, usend, urecv, fsend, frecv = scratch
    dp, s = lax.axis_index("dp"), lax.axis_index("seq")
    x, z = dp // n.Z, lax.rem(dp, n.Z)
    plane = x * n.S + s
    count = n.X * n.S
    mine = s * n.X + x
    blk, wide = n.blk, n.wide
    half = min(128, blk)
    gain = HEAD ** -0.5 * math.log2(math.e)
    bf, f32, i32 = jnp.bfloat16, jnp.float32, jnp.int32

    def done(ref, sem):
        pltpu.make_async_copy(ref, ref, sem).wait()

    def remote(src, dst, send, recv, dp_to, s_to):
        pltpu.make_async_remote_copy(
            src_ref=src, dst_ref=dst, send_sem=send, recv_sem=recv,
            device_id=(dp_to, s_to), device_id_type=MESH,
        ).start()

    def to_plane(body):
        for ds in range(1, n.S):
            body(x, lax.rem(s + ds, n.S))

        def one(dx, carry):
            xt = lax.rem(x + dx, n.X)
            for ds in range(n.S):
                body(xt, lax.rem(s + ds, n.S))
            return carry

        lax.fori_loop(1, n.X, one, 0)

    def z_of(place):
        return lax.rem(z - n.order[place] + n.Z, n.Z)

    def z_start(piece, place):
        zt = z if place == 0 else lax.rem(z + n.order[place], n.Z)
        hw = n.heads[piece] * HEAD
        first = pl.multiple_of(zt * n.qw + n.first_head[piece] * HEAD, HEAD)
        found = [(q_ref.at[:, pl.ds(first, hw)], zb[piece].at[place, :, pl.ds(0, hw)])]
        if piece == 0:
            cols = pl.ds(pl.multiple_of(zt * HEAD, HEAD), HEAD)
            found.append((k_ref.at[:, cols], zb[0].at[place, :, pl.ds(hw, HEAD)]))
            found.append((v_ref.at[:, cols], zb[0].at[place, :, pl.ds(hw + HEAD, HEAD)]))
        for src, dst in found:
            if place == 0:
                pltpu.make_async_copy(src, dst, zrecv.at[piece, 0]).start()
            else:
                remote(src, dst, zsend.at[piece, place], zrecv.at[piece, place], x * n.Z + zt, s)

    def iota(shape, dim):
        return lax.broadcasted_iota(i32, shape, dim)

    def exact(a, b, contract):
        high = jnp.floor(a * (1.0 / 16.0)) * 16.0
        dims = (contract, ((), ()))
        return lax.dot_general(high.astype(bf), b, dims, preferred_element_type=f32) + lax.dot_general(
            (a - high).astype(bf), b, dims, preferred_element_type=f32
        )

    def tables():
        groups, flat = n.groups, n.flat
        loads = [offsets_ref[pl.ds((x * n.Z + z_of(p)) * n.S + s, 1), :] for p in range(n.Z)]
        starts = jnp.concatenate(loads, axis=0).astype(f32)
        slot_lane, slot_sub = iota((1, flat), 1), iota((flat, 1), 0)
        owner = iota((flat, groups), 0) // n.slots
        of = iota((flat, groups), 1)
        same, after = (owner == of).astype(bf), (owner + 1 == of).astype(bf)
        nt = ((1,), (1,))
        for ref, slot, swap in ((idx_rows, slot_lane, False), (idx_cols, slot_sub, True)):
            pair = []
            for table in (same, after):
                if swap:
                    pair.append(lax.dot_general(table, starts.astype(bf), (nt, ((), ())), preferred_element_type=f32))
                else:
                    pair.append(lax.dot_general(starts.astype(bf), table, (nt, ((), ())), preferred_element_type=f32))
            begin = pair[0].astype(i32) + slot % n.slots
            end = pair[1].astype(i32) + jnp.where(slot // n.slots == groups - 1, n.tok, 0)
            ref[...] = jnp.where(begin < end, begin, -1)

        devices = n.X * n.Z * n.S
        column = iota((8, groups), 1)
        sign = jnp.where(column == plane + 1, 1.0, 0.0) - jnp.where(column == plane, 1.0, 0.0)
        counts = lax.dot_general(
            sign.astype(bf), offsets_ref[...].astype(f32).astype(bf), (nt, ((), ())), preferred_element_type=f32
        ) + jnp.where(plane == groups - 1, float(n.tok), 0.0)
        fa, fb_ = iota((devices, devices), 0), iota((devices, devices), 1)
        sa, sb_ = fa % n.S, fb_ % n.S
        few = counts.astype(bf)
        before = jnp.dot(few, ((sa == sb_) & (fa < fb_)).astype(bf), preferred_element_type=f32)
        totals = jnp.dot(few, (sa == sb_).astype(bf), preferred_element_type=f32)
        bases = jnp.dot(few, (sa < sb_).astype(bf), preferred_element_type=f32)

        pick_s = (iota((n.S, devices), 1) % n.S == iota((n.S, devices), 0)).astype(f32)
        cut = pick_s * before[0:1, :]
        cut_counts = pick_s * counts[0:1, :]
        flat_s = n.per_s
        at = iota((flat_s, devices), 0) // n.slots
        place = at % n.Z
        steps = (place + 1) // 2
        shift = jnp.where(place % 2 == 1, steps, n.Z - steps)
        z_at = (z - shift + 2 * n.Z) % n.Z
        line = (((at // n.Z) * n.Z + z_at) == iota((flat_s, devices), 1) // n.S).astype(bf)
        high = jnp.floor(cut * (1.0 / 16.0)) * 16.0
        three = [a.astype(bf) for a in (high, cut - high, cut_counts)]
        for ref, swap in ((dst_rows, False), (dst_cols, True)):
            got = []
            for a in three:
                pair = (line, a) if swap else (a, line)
                got.append(lax.dot_general(*pair, (nt, ((), ())), preferred_element_type=f32))
            slot = iota((flat_s, 1), 0) if swap else iota((1, flat_s), 1)
            slot = slot % n.slots
            ref[...] = jnp.where(slot < got[2].astype(i32), (got[0] + got[1]).astype(i32) + slot, -1)

        lens = jnp.broadcast_to(lengths_ref[pl.ds(plane, 1), :].astype(f32), (8, lengths_ref.shape[1]))
        docs = lengths_ref.shape[1]
        upto = (iota((docs, docs), 0) <= iota((docs, docs), 1)).astype(bf)
        ends = exact(lens, upto, ((1,), (0,)))[0:1, :].astype(i32)
        totals, bases = totals[0:1, :].astype(i32), bases[0:1, :].astype(i32)
        kind = iota((n.seg, HEAD), 1)
        kbuf[0 : n.pad, HEAD:] = (kind[0:1, :] == HEAD - 1).astype(bf) + jnp.zeros((n.pad, HEAD), bf)
        for k in range(n.S):
            tot, base = totals[:, k : k + 1], bases[:, k : k + 1]
            r = iota((n.seg, docs), 0)
            doc = jnp.sum(jnp.where(ends <= base + r, 1.0, 0.0), axis=1, keepdims=True)
            doc = jnp.broadcast_to(doc, (n.seg, HEAD)).astype(i32)
            real = iota((n.seg, HEAD), 0) < tot
            rows = slice(k * n.seg, (k + 1) * n.seg)
            qdoc[rows, :] = jnp.where(kind == jnp.where(real, doc, HEAD - 2), 0.0, APART).astype(bf)
            rows = slice(n.pad + k * n.seg, n.pad + (k + 1) * n.seg)
            kbuf[rows, HEAD:] = jnp.where(kind == jnp.where(real, doc, HEAD - 1), 1.0, 0.0).astype(bf)

    lane = iota((n.flat, n.tok), 1)

    def in_run(piece, run, after=None):
        first, last = n.in_runs[piece][run]
        for place in range(first, last):
            done(zb[piece].at[place], zrecv.at[piece, place])
            if after is not None and place:
                z_start(after, place)
            pick = (lane == idx_cols[:, place : place + 1]).astype(bf)
            padded = jnp.dot(pick, zb[piece][place], preferred_element_type=f32).astype(bf)
            sb[piece][:, place] = padded.reshape(n.groups, n.slots, n.widths[piece])
        run_of = pl.ds(first, last - first)
        pltpu.make_async_copy(sb[piece].at[plane, run_of], rc[piece].at[mine, run_of], precv.at[piece]).start()
        to_plane(
            lambda xt, st: remote(
                sb[piece].at[xt * n.S + st, run_of], rc[piece].at[mine, run_of],
                psend.at[piece, run], precv.at[piece], xt * n.Z + z, st,
            )
        )

    def compact(piece):
        done(rc[piece], precv.at[piece])
        sub = iota((n.seg, n.per_s), 0)
        hw = n.heads[piece] * HEAD
        for k in range(n.S):
            pick = (sub == dst_rows[k : k + 1, :]).astype(bf)
            block = rc[piece][k * n.X : (k + 1) * n.X].reshape(n.per_s, n.widths[piece])
            comp = jnp.dot(pick, block, preferred_element_type=f32).astype(bf)
            for h in range(n.heads[piece]):
                qbuf[piece][h, k * n.seg : (k + 1) * n.seg, :] = comp[:, h * HEAD : (h + 1) * HEAD]
            if piece == 0:
                at = n.pad + k * n.seg
                kbuf[at : at + n.seg, 0:HEAD] = comp[:, hw : hw + HEAD]
                vbuf[at : at + n.seg, 0:HEAD] = comp[:, hw + HEAD :]

    def attend(piece, i, rows):
        heads = n.heads[piece]
        start = pl.multiple_of(i * rows, rows)
        here = pl.ds(0, heads * rows)
        top[here, :] = jnp.full((heads * rows, half), NEG_FILL, f32)
        acc[here, :] = jnp.zeros((heads * rows, 2 * HEAD), f32)
        chunks = ((i + 1) * rows + wide - 1) // wide

        def at_keys(j):
            return pl.multiple_of((i + 1) * rows - wide * (j + 1) + n.pad, blk)

        def scores(j, diagonal):
            doc = qdoc[pl.ds(start, rows), :]
            queries = jnp.concatenate(
                [
                    qbuf[piece][:, pl.ds(start, rows), :].reshape(heads * rows, HEAD),
                    jnp.concatenate([doc] * heads, axis=0),
                ],
                axis=1,
            )
            sc = lax.dot_general(
                queries, kbuf[pl.ds(at_keys(j), wide), :], (((1,), (1,)), ((), ())), preferred_element_type=f32
            )
            best = top[here, :]
            for col in range(0, wide, half):
                part = sc[:, col : col + half]
                if diagonal and col >= wide - rows:
                    later = iota((rows, half), 1) + (col - wide + rows) > iota((rows, half), 0)
                    part = jnp.where(later[None], NEG_FILL, part.reshape(heads, rows, half)).reshape(
                        heads * rows, half
                    )
                strip[j, here, col : col + half] = part
                best = jnp.maximum(best, part)
            top[here, :] = best

        scores(0, True)

        def more(j, carry):
            scores(j, False)
            return carry

        lax.fori_loop(1, chunks, more, 0)
        top[here, :] = jnp.broadcast_to(jnp.max(top[here, :], axis=1, keepdims=True) * gain, (heads * rows, half))

        def weigh(j, carry):
            row = top[here, :]
            pieces = [
                jnp.exp2(strip[j, here, col : col + half] * gain - row).astype(bf) for col in range(0, wide, half)
            ]
            acc[here, :] += jnp.dot(
                jnp.concatenate(pieces, axis=1), vbuf[pl.ds(at_keys(j), wide), :], preferred_element_type=f32
            )
            return carry

        lax.fori_loop(0, chunks, weigh, 0)
        denom = acc[here, HEAD:]
        result = (acc[here, :HEAD] / jnp.where(denom > 0.0, denom, 1.0)).astype(bf)
        for h in range(heads):
            obuf[pl.ds(start, rows), h * HEAD : (h + 1) * HEAD] = result[h * rows : (h + 1) * rows]

    def out_all(piece):
        hw = n.heads[piece] * HEAD
        wide_lane = iota((n.per_s, n.seg), 1)
        for k in range(n.S):
            pick = (wide_lane == dst_cols[:, k : k + 1]).astype(bf)
            spread = jnp.dot(
                pick, obuf[k * n.seg : (k + 1) * n.seg, 0:hw], preferred_element_type=f32
            ).astype(bf)
            ub[piece][k] = spread.reshape(n.X, n.Z, n.slots, hw)
        for run, (first, last) in enumerate(n.out_runs[piece]):
            run_of = pl.ds(first, last - first)
            pltpu.make_async_copy(
                ub[piece].at[s, x, run_of], rb[piece].at[plane, run_of], urecv.at[piece, run]
            ).start()
            to_plane(
                lambda xt, st: remote(
                    ub[piece].at[st, xt, run_of], rb[piece].at[plane, run_of],
                    usend.at[piece, run], urecv.at[piece, run], xt * n.Z + z, st,
                )
            )

    tall = iota((n.tok, n.flat), 0)

    def hand_back(piece, run):
        first, last = n.out_runs[piece][run]
        hw = n.heads[piece] * HEAD
        done(rb[piece].at[:, pl.ds(first, last - first)], urecv.at[piece, run])
        cols = pl.ds(pl.multiple_of(z * n.qw + n.first_head[piece] * HEAD, HEAD), hw)
        for place in reversed(range(first, last)):
            pick = (tall == idx_rows[place : place + 1, :]).astype(bf)
            fb[piece][place] = jnp.dot(
                pick, rb[piece][:, place].reshape(n.flat, hw), preferred_element_type=f32
            ).astype(bf)
            if place == 0:
                pltpu.make_async_copy(fb[piece].at[0], out_ref.at[:, cols], frecv.at[piece, 0]).start()
            else:
                remote(
                    fb[piece].at[place], out_ref.at[:, cols],
                    fsend.at[piece, place], frecv.at[piece, place], x * n.Z + z_of(place), s,
                )

    for piece in range(2):
        z_start(piece, 0)
    greet(n, x, z, s)
    for place in range(1, n.Z):
        z_start(0, place)
    tables()
    kbuf[0 : n.pad, 0:HEAD] = jnp.zeros((n.pad, HEAD), bf)
    vbuf[:, 0:HEAD] = jnp.zeros((n.rows + n.pad, HEAD), bf)
    vbuf[:, HEAD:] = jnp.ones((n.rows + n.pad, HEAD), bf)

    for run in range(len(n.in_runs[0])):
        in_run(0, run, 1)
    compact(0)

    def with_runs(t, plan):
        for when, work in plan:

            @pl.when(t == when)
            def _(work=work):
                work()

    first_plan = [(2 + 3 * k, functools.partial(in_run, 1, k)) for k in range(len(n.in_runs[1]))]

    def first_block(t, carry):
        attend(0, t, blk)
        with_runs(t, first_plan)
        return carry

    lax.fori_loop(0, n.nb, first_block, 0)
    out_all(0)
    compact(1)
    second_plan = [(5 + 3 * k, functools.partial(hand_back, 0, k)) for k in range(min(2, len(n.out_runs[0])))]

    def second_block(t, carry):
        attend(1, t, blk)
        with_runs(t, second_plan)
        return carry

    lax.fori_loop(0, n.nb, second_block, 0)
    out_all(1)
    for run in range(2, len(n.out_runs[0])):
        hand_back(0, run)
    for run in range(len(n.out_runs[1])):
        hand_back(1, run)

    for piece in range(2):
        for place in range(n.Z):
            done(fb[piece].at[place], frecv.at[piece, place])
            if place:
                done(fb[piece].at[place], fsend.at[piece, place])
                done(zb[piece].at[place], zsend.at[piece, place])
        for run, (first, last) in enumerate(n.in_runs[piece]):
            done(sb[piece].at[pl.ds(0, count - 1), pl.ds(first, last - first)], psend.at[piece, run])
        for run, (first, last) in enumerate(n.out_runs[piece]):
            done(rb[piece].at[pl.ds(0, count - 1), pl.ds(first, last - first)], usend.at[piece, run])


def fused(n, offsets, lengths, q, k, v):
    vmem = pl.BlockSpec(memory_space=pltpu.VMEM)
    anyspace = pl.BlockSpec(memory_space=pl.ANY)
    half = min(128, n.blk)
    chunks = (n.nb + 3) // 4
    bf, f32 = jnp.bfloat16, jnp.float32
    sem = pltpu.SemaphoreType.DMA
    senders = n.X * n.S
    outs = [h * HEAD for h in n.heads]

    def each(widths, *dims):
        return [pltpu.VMEM(dims + (w,), bf) for w in widths]

    most = n.heads[0] * n.blk
    return pl.pallas_call(
        functools.partial(fused_kernel, n),
        out_shape=jax.ShapeDtypeStruct((n.tok, n.Z * n.qw), bf),
        in_specs=[vmem, vmem, anyspace, anyspace, anyspace],
        out_specs=vmem,
        scratch_shapes=each(n.widths, n.Z, n.tok)
        + each(n.widths, n.groups, n.Z, n.slots)
        + each(n.widths, senders, n.Z, n.slots)
        + [pltpu.VMEM((h, n.rows, HEAD), bf) for h in n.heads]
        + each(outs, n.S, n.X, n.Z, n.slots)
        + each(outs, n.groups, n.Z, n.slots)
        + each(outs, n.Z, n.tok)
        + [
            pltpu.VMEM((n.rows + n.pad, 2 * HEAD), bf),
            pltpu.VMEM((n.rows + n.pad, 2 * HEAD), bf),
            pltpu.VMEM((n.rows, HEAD), bf),
            pltpu.VMEM((chunks, most, n.wide), f32),
            pltpu.VMEM((most, half), f32),
            pltpu.VMEM((most, 2 * HEAD), f32),
            pltpu.VMEM((n.rows, outs[0]), bf),
            pltpu.VMEM((n.Z, n.flat), jnp.int32),
            pltpu.VMEM((n.flat, n.Z), jnp.int32),
            pltpu.VMEM((n.S, n.per_s), jnp.int32),
            pltpu.VMEM((n.per_s, n.S), jnp.int32),
            sem((2, n.Z)),
            sem((2, n.Z)),
            sem((2, 5)),
            sem((2,)),
            sem((2, 5)),
            sem((2, 5)),
            sem((2, n.Z)),
            sem((2, n.Z)),
        ],
        compiler_params=pltpu.CompilerParams(
            collective_id=0, has_side_effects=True, vmem_limit_bytes=VMEM_LIMIT
        ),
        name="route_and_attend",
    )(offsets, lengths, q, k, v)


def on_device(queries, keys, values, row_offsets, doc_lengths):
    n = Sizes(
        lax.axis_size("dp"), lax.axis_size("seq"), queries.shape[0], queries.shape[1], keys.shape[1],
        row_offsets.shape[1],
    )
    return fused(n, row_offsets, doc_lengths, queries, keys, values)


def solution(mesh):
    return jax.shard_map(
        on_device,
        mesh=mesh,
        in_specs=(P(("dp", "seq"), None), P(("dp", "seq"), None), P(("dp", "seq"), None), P(), P()),
        out_specs=P(("dp", "seq"), None),
        check_vma=False,
    )
```

```python
import functools
import math

import jax
import jax.numpy as jnp
from jax import lax
from jax.experimental import pallas as pl
from jax.experimental.pallas import tpu as pltpu
from jax.sharding import PartitionSpec as P

MESH = pl.DeviceIdType.MESH
HEAD = 128
NEG_FILL = -1e30
APART = -float(1 << 40)
VMEM_LIMIT = 50 * 1024 * 1024


class Sizes:
    def __init__(self, dp_count, seq_count, tok, width_q, width_k, groups):
        self.groups = groups
        self.S = seq_count
        self.Z = width_k // HEAD
        self.X = dp_count // self.Z
        self.tok = tok
        self.slots = 2 * tok // groups
        self.seg = 3 * dp_count * tok // (2 * groups)
        self.G = width_q // width_k
        self.qw = self.G * HEAD
        self.heads = (self.G // 2, self.G // 2)
        self.first_head = (0, self.G // 2)
        self.widths = (self.heads[0] * HEAD + 2 * HEAD, self.heads[1] * HEAD)
        self.flat = self.groups * self.slots
        self.per_s = self.X * self.Z * self.slots
        self.rows = self.S * self.seg
        self.blk = 2 * self.seg // 3
        self.nb = self.rows // self.blk
        self.pad = 3 * self.blk
        self.wide = 4 * self.blk
        order = [0]
        for dist in range(1, self.Z // 2 + 1):
            order.append(dist)
            if self.Z - dist != dist:
                order.append(self.Z - dist)
        self.order = order
        if self.Z == 8:
            fine = ((0, 1), (1, 3), (3, 5), (5, 7), (7, 8))
            self.in_runs = (fine, ((0, 3), (3, 5), (5, 8)))
            self.out_runs = (((5, 8), (3, 5), (0, 3)), ((7, 8), (5, 7), (3, 5), (0, 3)))
        else:
            runs = ((0, 1), (1, self.Z))
            self.in_runs = (runs,) * 2
            self.out_runs = (runs[::-1],) * 2


def greet(n, x, z, s):
    barrier = pltpu.get_barrier_semaphore()
    plane = x * n.S + s
    count = n.X * n.S

    def one_plane(t, carry):
        p = lax.rem(plane + t, count)
        pl.semaphore_signal(
            barrier, inc=1, device_id=((p // n.S) * n.Z + z, lax.rem(p, n.S)), device_id_type=MESH
        )
        return carry

    lax.fori_loop(1, count, one_plane, 0)

    def one_line(t, carry):
        zt = lax.rem(z + t, n.Z)
        pl.semaphore_signal(barrier, inc=1, device_id=(x * n.Z + zt, s), device_id_type=MESH)
        return carry

    lax.fori_loop(1, n.Z, one_line, 0)
    pl.semaphore_wait(barrier, count - 1 + n.Z - 1)


def fused_kernel(n, offsets_ref, lengths_ref, q_ref, k_ref, v_ref, out_ref, *scratch):
    scratch = list(scratch)

    def take(count):
        found = scratch[:count]
        del scratch[:count]
        return found

    zb, sb, rc, qbuf, ub, rb, fb = (take(2) for _ in range(7))
    kbuf, vbuf, qdoc, strip, top, acc, obuf, idx_rows, idx_cols, dst_rows, dst_cols = take(11)
    zsend, zrecv, psend, precv, usend, urecv, fsend, frecv = scratch
    dp, s = lax.axis_index("dp"), lax.axis_index("seq")
    x, z = dp // n.Z, lax.rem(dp, n.Z)
    plane = x * n.S + s
    count = n.X * n.S
    mine = s * n.X + x
    blk, wide = n.blk, n.wide
    half = min(128, blk)
    gain = HEAD ** -0.5 * math.log2(math.e)
    bf, f32, i32 = jnp.bfloat16, jnp.float32, jnp.int32

    def done(ref, sem):
        pltpu.make_async_copy(ref, ref, sem).wait()

    def remote(src, dst, send, recv, dp_to, s_to):
        pltpu.make_async_remote_copy(
            src_ref=src, dst_ref=dst, send_sem=send, recv_sem=recv,
            device_id=(dp_to, s_to), device_id_type=MESH,
        ).start()

    def to_plane(body):
        for ds in range(1, n.S):
            body(x, lax.rem(s + ds, n.S))

        def one(dx, carry):
            xt = lax.rem(x + dx, n.X)
            for ds in range(n.S):
                body(xt, lax.rem(s + ds, n.S))
            return carry

        lax.fori_loop(1, n.X, one, 0)

    def z_of(place):
        return lax.rem(z - n.order[place] + n.Z, n.Z)

    def z_start(piece, place):
        zt = z if place == 0 else lax.rem(z + n.order[place], n.Z)
        hw = n.heads[piece] * HEAD
        first = pl.multiple_of(zt * n.qw + n.first_head[piece] * HEAD, HEAD)
        found = [(q_ref.at[:, pl.ds(first, hw)], zb[piece].at[place, :, pl.ds(0, hw)])]
        if piece == 0:
            cols = pl.ds(pl.multiple_of(zt * HEAD, HEAD), HEAD)
            found.append((k_ref.at[:, cols], zb[0].at[place, :, pl.ds(hw, HEAD)]))
            found.append((v_ref.at[:, cols], zb[0].at[place, :, pl.ds(hw + HEAD, HEAD)]))
        for src, dst in found:
            if place == 0:
                pltpu.make_async_copy(src, dst, zrecv.at[piece, 0]).start()
            else:
                remote(src, dst, zsend.at[piece, place], zrecv.at[piece, place], x * n.Z + zt, s)

    def iota(shape, dim):
        return lax.broadcasted_iota(i32, shape, dim)

    def exact(a, b, contract):
        high = jnp.floor(a * (1.0 / 16.0)) * 16.0
        dims = (contract, ((), ()))
        return lax.dot_general(high.astype(bf), b, dims, preferred_element_type=f32) + lax.dot_general(
            (a - high).astype(bf), b, dims, preferred_element_type=f32
        )

    def tables():
        groups, flat = n.groups, n.flat
        devices = n.X * n.Z * n.S
        offsets = offsets_ref[...].astype(f32).astype(bf)
        which = iota((n.Z, devices), 0)
        steps = (which + 1) // 2
        which = (z - jnp.where(which % 2 == 1, steps, n.Z - steps) + 2 * n.Z) % n.Z
        line_of = (iota((n.Z, devices), 1) == (x * n.Z + which) * n.S + s).astype(bf)
        starts = lax.dot_general(line_of, offsets, (((1,), (1,)), ((), ())), preferred_element_type=f32)
        slot_lane, slot_sub = iota((1, flat), 1), iota((flat, 1), 0)
        owner = iota((flat, groups), 0) // n.slots
        of = iota((flat, groups), 1)
        same, after = (owner == of).astype(bf), (owner + 1 == of).astype(bf)
        nt = ((1,), (1,))
        for ref, slot, swap in ((idx_rows, slot_lane, False), (idx_cols, slot_sub, True)):
            pair = []
            for table in (same, after):
                if swap:
                    pair.append(lax.dot_general(table, starts.astype(bf), (nt, ((), ())), preferred_element_type=f32))
                else:
                    pair.append(lax.dot_general(starts.astype(bf), table, (nt, ((), ())), preferred_element_type=f32))
            begin = pair[0].astype(i32) + slot % n.slots
            end = pair[1].astype(i32) + jnp.where(slot // n.slots == groups - 1, n.tok, 0)
            ref[...] = jnp.where(begin < end, begin, -1)

        column = iota((8, groups), 1)
        sign = jnp.where(column == plane + 1, 1.0, 0.0) - jnp.where(column == plane, 1.0, 0.0)
        counts = lax.dot_general(
            sign.astype(bf), offsets, (((1,), (0,)), ((), ())), preferred_element_type=f32
        ) + jnp.where(plane == groups - 1, float(n.tok), 0.0)
        fa, fb_ = iota((devices, devices), 0), iota((devices, devices), 1)
        sa, sb_ = fa % n.S, fb_ % n.S
        few = counts.astype(bf)
        before = jnp.dot(few, ((sa == sb_) & (fa < fb_)).astype(bf), preferred_element_type=f32)
        totals = jnp.dot(few, (sa == sb_).astype(bf), preferred_element_type=f32)
        bases = jnp.dot(few, (sa < sb_).astype(bf), preferred_element_type=f32)

        pick_s = (iota((n.S, devices), 1) % n.S == iota((n.S, devices), 0)).astype(f32)
        cut = pick_s * before[0:1, :]
        cut_counts = pick_s * counts[0:1, :]
        flat_s = n.per_s
        at = iota((flat_s, devices), 0) // n.slots
        place = at % n.Z
        steps = (place + 1) // 2
        shift = jnp.where(place % 2 == 1, steps, n.Z - steps)
        z_at = (z - shift + 2 * n.Z) % n.Z
        line = (((at // n.Z) * n.Z + z_at) == iota((flat_s, devices), 1) // n.S).astype(bf)
        high = jnp.floor(cut * (1.0 / 16.0)) * 16.0
        three = [a.astype(bf) for a in (high, cut - high, cut_counts)]
        for ref, swap in ((dst_rows, False), (dst_cols, True)):
            got = []
            for a in three:
                pair = (line, a) if swap else (a, line)
                got.append(lax.dot_general(*pair, (nt, ((), ())), preferred_element_type=f32))
            slot = iota((flat_s, 1), 0) if swap else iota((1, flat_s), 1)
            slot = slot % n.slots
            ref[...] = jnp.where(slot < got[2].astype(i32), (got[0] + got[1]).astype(i32) + slot, -1)

        lens = jnp.broadcast_to(lengths_ref[pl.ds(plane, 1), :].astype(f32), (8, lengths_ref.shape[1]))
        docs = lengths_ref.shape[1]
        upto = (iota((docs, docs), 0) <= iota((docs, docs), 1)).astype(bf)
        ends = exact(lens, upto, ((1,), (0,)))[0:1, :].astype(i32)
        totals, bases = totals[0:1, :].astype(i32), bases[0:1, :].astype(i32)
        kind = iota((n.seg, HEAD), 1)
        kbuf[0 : n.pad, HEAD:] = (kind[0:1, :] == HEAD - 1).astype(bf) + jnp.zeros((n.pad, HEAD), bf)
        for k in range(n.S):
            tot, base = totals[:, k : k + 1], bases[:, k : k + 1]
            r = iota((n.seg, docs), 0)
            doc = jnp.sum(jnp.where(ends <= base + r, 1.0, 0.0), axis=1, keepdims=True)
            doc = jnp.broadcast_to(doc, (n.seg, HEAD)).astype(i32)
            real = iota((n.seg, HEAD), 0) < tot
            rows = slice(k * n.seg, (k + 1) * n.seg)
            qdoc[rows, :] = jnp.where(kind == jnp.where(real, doc, HEAD - 2), 0.0, APART).astype(bf)
            rows = slice(n.pad + k * n.seg, n.pad + (k + 1) * n.seg)
            kbuf[rows, HEAD:] = jnp.where(kind == jnp.where(real, doc, HEAD - 1), 1.0, 0.0).astype(bf)

    lane = iota((n.flat, n.tok), 1)

    def in_run(piece, run, after=None):
        first, last = n.in_runs[piece][run]
        for place in range(first, last):
            done(zb[piece].at[place], zrecv.at[piece, place])
            if after is not None and place:
                z_start(after, place)
            pick = (lane == idx_cols[:, place : place + 1]).astype(bf)
            padded = jnp.dot(pick, zb[piece][place], preferred_element_type=f32).astype(bf)
            sb[piece][:, place] = padded.reshape(n.groups, n.slots, n.widths[piece])
        run_of = pl.ds(first, last - first)
        pltpu.make_async_copy(sb[piece].at[plane, run_of], rc[piece].at[mine, run_of], precv.at[piece]).start()
        to_plane(
            lambda xt, st: remote(
                sb[piece].at[xt * n.S + st, run_of], rc[piece].at[mine, run_of],
                psend.at[piece, run], precv.at[piece], xt * n.Z + z, st,
            )
        )

    def compact(piece):
        done(rc[piece], precv.at[piece])
        sub = iota((n.seg, n.per_s), 0)
        hw = n.heads[piece] * HEAD
        for k in range(n.S):
            pick = (sub == dst_rows[k : k + 1, :]).astype(bf)
            block = rc[piece][k * n.X : (k + 1) * n.X].reshape(n.per_s, n.widths[piece])
            comp = jnp.dot(pick, block, preferred_element_type=f32).astype(bf)
            for h in range(n.heads[piece]):
                qbuf[piece][h, k * n.seg : (k + 1) * n.seg, :] = comp[:, h * HEAD : (h + 1) * HEAD]
            if piece == 0:
                at = n.pad + k * n.seg
                kbuf[at : at + n.seg, 0:HEAD] = comp[:, hw : hw + HEAD]
                vbuf[at : at + n.seg, 0:HEAD] = comp[:, hw + HEAD :]

    def attend(piece, i, rows):
        heads = n.heads[piece]
        start = pl.multiple_of(i * rows, rows)
        here = pl.ds(0, heads * rows)
        top[here, :] = jnp.full((heads * rows, half), NEG_FILL, f32)
        acc[here, :] = jnp.zeros((heads * rows, 2 * HEAD), f32)
        chunks = ((i + 1) * rows + wide - 1) // wide

        def at_keys(j):
            return pl.multiple_of((i + 1) * rows - wide * (j + 1) + n.pad, blk)

        def scores(j, diagonal):
            doc = qdoc[pl.ds(start, rows), :]
            queries = jnp.concatenate(
                [
                    qbuf[piece][:, pl.ds(start, rows), :].reshape(heads * rows, HEAD),
                    jnp.concatenate([doc] * heads, axis=0),
                ],
                axis=1,
            )
            sc = lax.dot_general(
                queries, kbuf[pl.ds(at_keys(j), wide), :], (((1,), (1,)), ((), ())), preferred_element_type=f32
            )
            best = top[here, :]
            for col in range(0, wide, half):
                part = sc[:, col : col + half]
                if diagonal and col >= wide - rows:
                    later = iota((rows, half), 1) + (col - wide + rows) > iota((rows, half), 0)
                    part = jnp.where(later[None], NEG_FILL, part.reshape(heads, rows, half)).reshape(
                        heads * rows, half
                    )
                strip[j, here, col : col + half] = part
                best = jnp.maximum(best, part)
            top[here, :] = best

        scores(0, True)

        def more(j, carry):
            scores(j, False)
            return carry

        lax.fori_loop(1, chunks, more, 0)
        top[here, :] = jnp.broadcast_to(jnp.max(top[here, :], axis=1, keepdims=True) * gain, (heads * rows, half))

        def weigh(j, carry):
            row = top[here, :]
            pieces = [
                jnp.exp2(strip[j, here, col : col + half] * gain - row).astype(bf) for col in range(0, wide, half)
            ]
            acc[here, :] += jnp.dot(
                jnp.concatenate(pieces, axis=1), vbuf[pl.ds(at_keys(j), wide), :], preferred_element_type=f32
            )
            return carry

        lax.fori_loop(0, chunks, weigh, 0)
        denom = acc[here, HEAD:]
        result = (acc[here, :HEAD] / jnp.where(denom > 0.0, denom, 1.0)).astype(bf)
        for h in range(heads):
            obuf[pl.ds(start, rows), h * HEAD : (h + 1) * HEAD] = result[h * rows : (h + 1) * rows]

    def out_all(piece):
        hw = n.heads[piece] * HEAD
        wide_lane = iota((n.per_s, n.seg), 1)
        for k in range(n.S):
            pick = (wide_lane == dst_cols[:, k : k + 1]).astype(bf)
            spread = jnp.dot(
                pick, obuf[k * n.seg : (k + 1) * n.seg, 0:hw], preferred_element_type=f32
            ).astype(bf)
            ub[piece][k] = spread.reshape(n.X, n.Z, n.slots, hw)
        for run, (first, last) in enumerate(n.out_runs[piece]):
            run_of = pl.ds(first, last - first)
            pltpu.make_async_copy(
                ub[piece].at[s, x, run_of], rb[piece].at[plane, run_of], urecv.at[piece, run]
            ).start()
            to_plane(
                lambda xt, st: remote(
                    ub[piece].at[st, xt, run_of], rb[piece].at[plane, run_of],
                    usend.at[piece, run], urecv.at[piece, run], xt * n.Z + z, st,
                )
            )

    tall = iota((n.tok, n.flat), 0)

    def hand_back(piece, run):
        first, last = n.out_runs[piece][run]
        hw = n.heads[piece] * HEAD
        done(rb[piece].at[:, pl.ds(first, last - first)], urecv.at[piece, run])
        cols = pl.ds(pl.multiple_of(z * n.qw + n.first_head[piece] * HEAD, HEAD), hw)
        for place in reversed(range(first, last)):
            pick = (tall == idx_rows[place : place + 1, :]).astype(bf)
            fb[piece][place] = jnp.dot(
                pick, rb[piece][:, place].reshape(n.flat, hw), preferred_element_type=f32
            ).astype(bf)
            if place == 0:
                pltpu.make_async_copy(fb[piece].at[0], out_ref.at[:, cols], frecv.at[piece, 0]).start()
            else:
                remote(
                    fb[piece].at[place], out_ref.at[:, cols],
                    fsend.at[piece, place], frecv.at[piece, place], x * n.Z + z_of(place), s,
                )

    for piece in range(2):
        z_start(piece, 0)
    greet(n, x, z, s)
    for place in range(1, n.Z):
        z_start(0, place)
    tables()
    kbuf[0 : n.pad, 0:HEAD] = jnp.zeros((n.pad, HEAD), bf)
    vbuf[:, 0:HEAD] = jnp.zeros((n.rows + n.pad, HEAD), bf)
    vbuf[:, HEAD:] = jnp.ones((n.rows + n.pad, HEAD), bf)

    for run in range(len(n.in_runs[0])):
        in_run(0, run, 1)
    compact(0)

    def with_runs(t, plan):
        for when, work in plan:

            @pl.when(t == when)
            def _(work=work):
                work()

    first_plan = [(2 + 3 * k, functools.partial(in_run, 1, k)) for k in range(len(n.in_runs[1]))]

    def first_block(t, carry):
        attend(0, t, blk)
        with_runs(t, first_plan)
        return carry

    lax.fori_loop(0, n.nb, first_block, 0)
    out_all(0)
    compact(1)
    second_plan = [(5 + 3 * k, functools.partial(hand_back, 0, k)) for k in range(min(2, len(n.out_runs[0])))]

    def second_block(t, carry):
        attend(1, t, blk)
        with_runs(t, second_plan)
        return carry

    lax.fori_loop(0, n.nb, second_block, 0)
    out_all(1)
    for run in range(2, len(n.out_runs[0])):
        hand_back(0, run)
    for run in range(len(n.out_runs[1])):
        hand_back(1, run)

    for piece in range(2):
        for place in range(n.Z):
            done(fb[piece].at[place], frecv.at[piece, place])
            if place:
                done(fb[piece].at[place], fsend.at[piece, place])
                done(zb[piece].at[place], zsend.at[piece, place])
        for run, (first, last) in enumerate(n.in_runs[piece]):
            done(sb[piece].at[pl.ds(0, count - 1), pl.ds(first, last - first)], psend.at[piece, run])
        for run, (first, last) in enumerate(n.out_runs[piece]):
            done(rb[piece].at[pl.ds(0, count - 1), pl.ds(first, last - first)], usend.at[piece, run])


def fused(n, offsets, lengths, q, k, v):
    vmem = pl.BlockSpec(memory_space=pltpu.VMEM)
    anyspace = pl.BlockSpec(memory_space=pl.ANY)
    half = min(128, n.blk)
    chunks = (n.nb + 3) // 4
    bf, f32 = jnp.bfloat16, jnp.float32
    sem = pltpu.SemaphoreType.DMA
    senders = n.X * n.S
    outs = [h * HEAD for h in n.heads]

    def each(widths, *dims):
        return [pltpu.VMEM(dims + (w,), bf) for w in widths]

    most = n.heads[0] * n.blk
    return pl.pallas_call(
        functools.partial(fused_kernel, n),
        out_shape=jax.ShapeDtypeStruct((n.tok, n.Z * n.qw), bf),
        in_specs=[vmem, vmem, anyspace, anyspace, anyspace],
        out_specs=anyspace,
        scratch_shapes=each(n.widths, n.Z, n.tok)
        + each(n.widths, n.groups, n.Z, n.slots)
        + each(n.widths, senders, n.Z, n.slots)
        + [pltpu.VMEM((h, n.rows, HEAD), bf) for h in n.heads]
        + each(outs, n.S, n.X, n.Z, n.slots)
        + each(outs, n.groups, n.Z, n.slots)
        + each(outs, n.Z, n.tok)
        + [
            pltpu.VMEM((n.rows + n.pad, 2 * HEAD), bf),
            pltpu.VMEM((n.rows + n.pad, 2 * HEAD), bf),
            pltpu.VMEM((n.rows, HEAD), bf),
            pltpu.VMEM((chunks, most, n.wide), f32),
            pltpu.VMEM((most, half), f32),
            pltpu.VMEM((most, 2 * HEAD), f32),
            pltpu.VMEM((n.rows, outs[0]), bf),
            pltpu.VMEM((n.Z, n.flat), jnp.int32),
            pltpu.VMEM((n.flat, n.Z), jnp.int32),
            pltpu.VMEM((n.S, n.per_s), jnp.int32),
            pltpu.VMEM((n.per_s, n.S), jnp.int32),
            sem((2, n.Z)),
            sem((2, n.Z)),
            sem((2, 5)),
            sem((2,)),
            sem((2, 5)),
            sem((2, 5)),
            sem((2, n.Z)),
            sem((2, n.Z)),
        ],
        compiler_params=pltpu.CompilerParams(
            collective_id=0, has_side_effects=True, vmem_limit_bytes=VMEM_LIMIT
        ),
        name="route_and_attend",
    )(offsets, lengths, q, k, v)


def on_device(queries, keys, values, row_offsets, doc_lengths):
    n = Sizes(
        lax.axis_size("dp"), lax.axis_size("seq"), queries.shape[0], queries.shape[1], keys.shape[1],
        row_offsets.shape[1],
    )
    return fused(n, jnp.transpose(row_offsets), doc_lengths, queries, keys, values)


def solution(mesh):
    return jax.shard_map(
        on_device,
        mesh=mesh,
        in_specs=(P(("dp", "seq"), None), P(("dp", "seq"), None), P(("dp", "seq"), None), P(), P()),
        out_specs=P(("dp", "seq"), None),
        check_vma=False,
    )
```
